128 devices in a mesh: row: 8 (over x, core), col: 16 (over y, z).
Axes of the slice: x: 4, y: 4, z: 4, core: 2. Of those that a mesh axis runs over, the one named last changes fastest.
Arguments:
- latent: bfloat16 [384, 512, 640], P('row', 'col'), may hold values from -260 to 260
- blend: int32 [384, 512], P('row', 'col'), may hold values from 1 to 3
- gamma_local: float32 [640], replicated, may hold values from 0.5 to 1.5
- beta_local: float32 [640], replicated, may hold values from -3 to 3
- kernel_local: bfloat16 [3, 3, 640, 640], replicated, may hold values from -0.078125 to 0.078125
- bias_local: float32 [640], replicated, may hold values from -3 to 3
- gamma_dilated: float32 [640], replicated, may hold values from 0.5 to 1.5
- beta_dilated: float32 [640], replicated, may hold values from -3 to 3
- kernel_dilated: bfloat16 [3, 3, 640, 640], replicated, may hold values from -0.078125 to 0.078125
- bias_dilated: float32 [640], replicated, may hold values from -3 to 3
Outputs:
- blended: bfloat16 [384, 512, 640], P('row', 'col')
The draws below stay inside these ranges and needn't reach their ends.
All inputs are finite; a program needn't handle non-finite values.
Results may differ from the reference program's by a relative error of at most 0.0052.
Values may be sent and summed in bfloat16 or wider, within the bound.
A program may use at most 192 MiB of HBM per device.

```python
import math
import jax
import jax.numpy as jnp
from jax import lax

CH = 640
GROUPS = 32
STRIDE = 4
HEIGHT = 384
WIDTH = 512


def draw_latent(key, part):
    key = jax.random.fold_in(key, 11)
    key_base, key_rows, key_cols, key_chan, key_texture, key_blocks = jax.random.split(key, 6)
    row_pos = jnp.arange(HEIGHT).astype(jnp.float32) / HEIGHT
    col_pos = jnp.arange(WIDTH).astype(jnp.float32) / WIDTH
    row_scale = jnp.power(3.0, row_pos) * jax.random.uniform(key_rows, (HEIGHT,), jnp.float32, 0.7, 1.2)
    col_scale = jnp.power(3.0, col_pos) * jax.random.uniform(key_cols, (WIDTH,), jnp.float32, 0.7, 1.2)
    texture_table = jnp.exp(jax.random.uniform(key_texture, (8, 8), jnp.float32, math.log(0.15), math.log(1.5)))
    row_ids = jnp.arange(HEIGHT) % 8
    col_ids = jnp.arange(WIDTH) % 8
    texture = texture_table[row_ids][:, col_ids]
    block_table = jnp.exp(jax.random.uniform(key_blocks, ((HEIGHT + 7) // 8, (WIDTH + 7) // 8), jnp.float32, math.log(0.3), 0.0))
    block_scale = block_table[jnp.arange(HEIGHT) // 8][:, jnp.arange(WIDTH) // 8]
    base = jnp.clip(jax.random.normal(key_base, (HEIGHT, WIDTH, CH), jnp.float32), -4.5, 4.5)
    offset = 0.4 + 0.3 * (row_pos[:, None] + col_pos[None, :])
    chan_scale = jnp.exp(jax.random.uniform(key_chan, (CH,), jnp.float32, math.log(0.5), math.log(2.0)))
    cell_scale = row_scale[:, None] * col_scale[None, :] * texture * block_scale
    values = (base + offset[:, :, None]) * cell_scale[:, :, None] * chan_scale[None, None, :]
    return values.astype(jnp.bfloat16)


def place_ends(values, stream_key, smallest, largest):
    spot = [jax.random.randint(jax.random.fold_in(stream_key, axis), (), 0, length) for axis, length in enumerate(values.shape)]
    longest = values.shape.index(max(values.shape))
    beside = spot[:longest] + [(spot[longest] + 1) % values.shape[longest]] + spot[longest + 1:]
    return values.at[tuple(spot)].set(smallest).at[tuple(beside)].set(largest)


def normal_values(rng, dims, scale, limit, dtype=jnp.bfloat16):
    array = scale * jax.random.normal(rng, dims, jnp.float32)
    return jnp.clip(array, min=-limit, max=limit).astype(dtype)


def setup_inputs(seed: int = 0) -> dict:
    seeds = jax.random.split(jax.random.key(seed), 11)
    latent = draw_latent(jax.random.fold_in(seeds[10], 71), 0)
    blend = place_ends(jax.random.randint(seeds[1], (HEIGHT, WIDTH), 1, 4), jax.random.fold_in(seeds[1], 1), 1, 3).astype(jnp.int32)
    gamma_local = jnp.clip(jax.random.uniform(seeds[2], (CH,), jnp.float32, 0.5, 1.5), 0.5, 1.5)
    beta_local = normal_values(seeds[3], (CH,), 0.5, 3.0, jnp.float32)
    kernel_local = normal_values(seeds[4], (3, 3, CH, CH), (9 * CH) ** -0.5, 0.078125)
    bias_local = normal_values(seeds[5], (CH,), 0.5, 3.0, jnp.float32)
    gamma_dilated = jnp.clip(jax.random.uniform(seeds[6], (CH,), jnp.float32, 0.5, 1.5), 0.5, 1.5)
    beta_dilated = normal_values(seeds[7], (CH,), 0.5, 3.0, jnp.float32)
    kernel_dilated = normal_values(seeds[8], (3, 3, CH, CH), (9 * CH) ** -0.5, 0.078125)
    bias_dilated = normal_values(seeds[9], (CH,), 0.5, 3.0, jnp.float32)
    return dict(latent=latent, blend=blend, gamma_local=gamma_local, beta_local=beta_local, kernel_local=kernel_local, bias_local=bias_local, gamma_dilated=gamma_dilated, beta_dilated=beta_dilated, kernel_dilated=kernel_dilated, bias_dilated=bias_dilated)


def convolve(act, kernel, step):
    out = lax.conv_general_dilated(act[None], kernel, (1, 1), [(step, step), (step, step)], rhs_dilation=(step, step), dimension_numbers=('NHWC', 'HWIO', 'NHWC'), preferred_element_type=jnp.float32)
    return out[0]

def reference(latent, blend, gamma_local, beta_local, kernel_local, bias_local, gamma_dilated, beta_dilated, kernel_dilated, bias_dilated):
    x = latent.astype(jnp.float32)
    height, width, chans = x.shape
    per_group = chans // GROUPS
    grouped = x.reshape(height, width, GROUPS, per_group)
    mean_local = lax.optimization_barrier(jnp.mean(grouped, axis=(0, 1, 3)))
    centered = grouped - mean_local[:, None]
    var_local = lax.optimization_barrier(jnp.mean(centered * centered, axis=(0, 1, 3)))
    normed = (centered * lax.rsqrt(var_local + 1e-05)[:, None]).reshape(height, width, chans)
    act_local = jax.nn.silu(normed * gamma_local + beta_local).astype(jnp.bfloat16)
    subs = x.reshape(height // STRIDE, STRIDE, width // STRIDE, STRIDE, GROUPS, per_group)
    mean_sub = lax.optimization_barrier(jnp.mean(subs, axis=(0, 2, 5)))
    centered_sub = subs - mean_sub[None, :, None, :, :, None]
    var_sub = lax.optimization_barrier(jnp.mean(centered_sub * centered_sub, axis=(0, 2, 5)))
    normed_sub = (centered_sub * lax.rsqrt(var_sub + 1e-05)[None, :, None, :, :, None]).reshape(height, width, chans)
    act_dilated = jax.nn.silu(normed_sub * gamma_dilated + beta_dilated).astype(jnp.bfloat16)
    local = convolve(act_local, kernel_local, 1) + bias_local
    dilated = (convolve(act_dilated, kernel_dilated, STRIDE) + bias_dilated).astype(jnp.bfloat16)
    weight = blend.astype(jnp.float32)[:, :, None]
    mixed = (weight * local + (4.0 - weight) * dilated.astype(jnp.float32)) * 0.25
    return mixed.astype(jnp.bfloat16)
```

```python
import jax
import jax.numpy as jnp
from jax import lax
from jax.experimental import pallas as pl
from jax.experimental.pallas import tpu as pltpu
from jax.sharding import PartitionSpec as P

CH = 640
GROUPS = 32
PER_GROUP = 20
ROWS = 48
COLS = 32
PAIRS = ROWS // 2
KDIM = 3 * CH
F32 = jnp.float32
BF16 = jnp.bfloat16
MESH = pl.DeviceIdType.MESH
NROW = 8
NCOL = 16
LOCAL_COUNT = float((ROWS // 4) * (COLS // 4) * PER_GROUP)


def groups_to_lanes(part):
    chan = lax.broadcasted_iota(jnp.int32, (CH, 128), 0)
    lane = lax.broadcasted_iota(jnp.int32, (CH, 128), 1) - GROUPS * part
    first = lane * PER_GROUP
    return jnp.where((lane >= 0) & (chan >= first) & (chan < first + PER_GROUP), 1.0, 0.0).astype(F32)


def lanes_to_channels(part):
    lane = lax.broadcasted_iota(jnp.int32, (128, CH), 0) - GROUPS * part
    chan = lax.broadcasted_iota(jnp.int32, (128, CH), 1)
    first = lane * PER_GROUP
    return jnp.where((lane >= 0) & (chan >= first) & (chan < first + PER_GROUP), 1.0, 0.0).astype(F32)


def exact_dot(a, b):
    return lax.dot_general(
        a, b, (((1,), (0,)), ((), ())), precision=lax.Precision.HIGHEST, preferred_element_type=F32
    )


def fold_half(tile):
    return tile + pltpu.roll(tile, 4, 0)


def merge(tiles, count):
    number = len(tiles)
    average = tiles[0]
    for tile in tiles[1:]:
        average = average + tile
    total = average
    average = average * (1.0 / number)
    spread = None
    for tile in tiles:
        gap = tile - average
        spread = gap * gap if spread is None else spread + gap * gap
    rows = lax.broadcasted_iota(jnp.int32, (8, 128), 0)
    return jnp.where(rows < 4, average, total + count * pltpu.roll(spread, 4, 0))


def gather_kernel(
    lat_hbm, kl_hbm, kd_hbm, blend_ref,
    lat, top, bot, left, right, stats, wl, wd, wgt,
    mid_l, mid_d, strip_l, strip_r, tile1, tile2, got1, got2,
    sem_in, sem_w, send_h, recv_h, send1, recv1, send2, recv2,
):
    row = lax.axis_index("row")
    col = lax.axis_index("col")
    has_up = row > 0
    has_dn = row < NROW - 1
    has_lf = col > 0
    has_rt = col < NCOL - 1

    load = pltpu.make_async_copy(lat_hbm, lat, sem_in)
    load.start()
    weights = []
    for n, (src, planes, mid) in enumerate(((kd_hbm, wd, mid_d), (kl_hbm, wl, mid_l))):
        for m, (a, dst) in enumerate(((0, planes.at[0]), (1, mid), (2, planes.at[3]))):
            copy = pltpu.make_async_copy(src.at[a], dst, sem_w.at[3 * n + m])
            copy.start()
            weights.append(copy)

    barrier = pltpu.get_barrier_semaphore()
    for d in range(1, NROW):
        pl.semaphore_signal(barrier, 1, device_id=(lax.rem(row + d, NROW), col), device_id_type=MESH)
    for d in range(1, NCOL):
        pl.semaphore_signal(barrier, 1, device_id=(row, lax.rem(col + d, NCOL)), device_id_type=MESH)
    for dr, okr in ((-1, has_up), (1, has_dn)):
        for dc, okc in ((-1, has_lf), (1, has_rt)):
            @pl.when(okr & okc)
            def _():
                pl.semaphore_signal(barrier, 1, device_id=(row + dr, col + dc), device_id_type=MESH)

    load.wait()

    @pl.loop(0, ROWS // 4)
    def _(k):
        for strip, start, part in ((strip_l, 0, 0), (strip_r, 16, 12)):
            pieces = [
                lat[4 * k + p, pl.ds(start, 16), :].astype(F32)[part : part + 4] for p in range(4)
            ]
            strip[k] = jnp.concatenate(pieces, axis=0).astype(BF16)

    diagonals = (jnp.where(has_up, 1, 0) + jnp.where(has_dn, 1, 0)) * (
        jnp.where(has_lf, 1, 0) + jnp.where(has_rt, 1, 0)
    )
    pl.semaphore_wait(barrier, NROW - 1 + NCOL - 1 + diagonals)

    last = ROWS // 4 - 1
    halos = []
    for n, (src, dst, dr, dc, ok, got) in enumerate((
        (lat.at[pl.ds(ROWS - 4, 4)], top, 1, 0, has_dn, has_up),
        (lat.at[pl.ds(0, 4)], bot, -1, 0, has_up, has_dn),
        (strip_r, left.at[pl.ds(1, ROWS // 4)], 0, 1, has_rt, has_lf),
        (strip_l, right.at[pl.ds(1, ROWS // 4)], 0, -1, has_lf, has_rt),
        (strip_r.at[last], left.at[0], 1, 1, has_dn & has_rt, has_up & has_lf),
        (strip_r.at[0], left.at[ROWS // 4 + 1], -1, 1, has_up & has_rt, has_dn & has_lf),
        (strip_l.at[last], right.at[0], 1, -1, has_dn & has_lf, has_up & has_rt),
        (strip_l.at[0], right.at[ROWS // 4 + 1], -1, -1, has_up & has_lf, has_dn & has_rt),
    )):
        copy = pltpu.make_async_remote_copy(
            src_ref=src, dst_ref=dst, send_sem=send_h.at[n], recv_sem=recv_h.at[n],
            device_id=(row + dr, col + dc), device_id_type=MESH,
        )
        halos.append((copy, ok, got))

    def sums(k, acc):
        out = []
        for p in range(4):
            x = lat[4 * k + p].astype(F32)
            out.append(acc[p] + ((x[0:8] + x[8:16]) + (x[16:24] + x[24:32])))
        return tuple(out)

    zero = tuple(jnp.zeros((8, CH), F32) for _ in range(4))
    acc = lax.fori_loop(0, ROWS // 4, sums, zero)
    mean = None
    for p in range(4):
        term = exact_dot(acc[p], groups_to_lanes(p))
        mean = term if mean is None else mean + term
    mean = fold_half(mean) * (1.0 / LOCAL_COUNT)
    centre = [exact_dot(mean, lanes_to_channels(p)) for p in range(4)]

    def squares(k, acc):
        out = []
        for p in range(4):
            x = lat[4 * k + p].astype(F32)
            term = None
            for s in range(4):
                gap = x[8 * s : 8 * s + 8] - centre[p]
                term = gap * gap if term is None else term + gap * gap
            out.append(acc[p] + term)
        return tuple(out)

    acc = lax.fori_loop(0, ROWS // 4, squares, zero)
    square = None
    for p in range(4):
        term = exact_dot(acc[p], groups_to_lanes(p))
        square = term if square is None else square + term
    square = fold_half(square)
    rows8 = lax.broadcasted_iota(jnp.int32, (8, 128), 0)
    tile1[...] = jnp.where(rows8 < 4, mean, square)

    first = []
    for d in range(1, NROW):
        copy = pltpu.make_async_remote_copy(
            src_ref=tile1, dst_ref=got1.at[d], send_sem=send1.at[d], recv_sem=recv1.at[d],
            device_id=(lax.rem(row + d, NROW), col), device_id_type=MESH,
        )
        copy.start()
        first.append(copy)

    for copy, ok, _ in halos:
        @pl.when(ok)
        def _():
            copy.start()

    def planes(dst, mid):
        @pl.loop(0, KDIM // 32)
        def _(i):
            at = pl.ds(pl.multiple_of(i * 32, 32), 32)
            ends = dst[0, at, :].astype(F32) + dst[3, at, :].astype(F32)
            centre_tap = mid[at, :].astype(F32)
            dst[1, at, :] = ((ends + centre_tap) * 0.5).astype(BF16)
            dst[2, at, :] = ((ends - centre_tap) * 0.5).astype(BF16)

    share = blend_ref[...].astype(F32) * 0.25
    turned = share.T
    for r in range(ROWS):
        wgt[pl.ds(r * COLS, COLS), :] = jnp.broadcast_to(turned[:, r : r + 1], (COLS, 128))

    for copy in first:
        copy.wait_recv()
    tile2[...] = merge([tile1[...]] + [got1[d] for d in range(1, NROW)], LOCAL_COUNT)
    second = []
    for d in range(1, NCOL):
        copy = pltpu.make_async_remote_copy(
            src_ref=tile2, dst_ref=got2.at[d], send_sem=send2.at[d], recv_sem=recv2.at[d],
            device_id=(row, lax.rem(col + d, NCOL)), device_id_type=MESH,
        )
        copy.start()
        second.append(copy)

    for copy in weights[:3]:
        copy.wait()
    planes(wd, mid_d)
    for copy in weights[3:]:
        copy.wait()
    planes(wl, mid_l)

    for copy in second:
        copy.wait_recv()
    count = LOCAL_COUNT * NROW
    tile = merge([tile2[...]] + [got2[d] for d in range(1, NCOL)], count)
    count = count * NCOL
    mean = jnp.where(rows8 < 4, tile, pltpu.roll(tile, 4, 0))
    square = jnp.where(rows8 < 4, pltpu.roll(tile, 4, 0), tile)

    def everywhere(v):
        for step in (1, 2, 4):
            v = v + pltpu.roll(v, step, 0)
        for step in (32, 64):
            v = v + pltpu.roll(v, step, 1)
        return v * (1.0 / 32.0)

    mean_all = everywhere(mean)
    gap = mean - mean_all
    var_all = everywhere(square * (1.0 / count) + gap * gap)
    var = square * (1.0 / count)
    stats[pl.ds(0, 8)] = mean
    stats[pl.ds(8, 8)] = lax.rsqrt(var + 1e-05)
    stats[pl.ds(16, 8)] = mean_all
    stats[pl.ds(24, 8)] = lax.rsqrt(var_all + 1e-05)

    for copy, ok, got in halos:
        @pl.when(got)
        def _():
            copy.wait_recv()

        @pl.when(ok)
        def _():
            copy.wait_send()
    for copy in first + second:
        copy.wait_send()


def conv_kernel(
    lat, top, bot, left, right, stats, wl, wd, wgt,
    gam_l, bet_l, bia_l, gam_d, bet_d, bia_d,
    out,
    act_l, act_d, lhs, sum_l, sum_d, scale_d, shift_d, scale_e, shift_e,
):
    row = lax.axis_index("row")
    col = lax.axis_index("col")
    has_up = row > 0
    has_dn = row < NROW - 1
    has_lf = col > 0
    has_rt = col < NCOL - 1

    half = 0.5
    for p in range(4):
        spread = exact_dot(stats[pl.ds(0, 16)], lanes_to_channels(p))
        scale = spread[8:16] * (gam_d[...] * half)
        shift = bet_d[...] * half - spread[0:8] * scale
        scale_d[p] = scale
        shift_d[p] = shift
        scale_e[pl.ds(4 * p, 4)] = scale[0:4]
        shift_e[pl.ds(4 * p, 4)] = shift[0:4]
    spread = exact_dot(stats[pl.ds(16, 16)], lanes_to_channels(0))
    scale_l = spread[8:16] * (gam_l[...] * half)
    shift_l = bet_l[...] * half - spread[0:8] * scale_l

    def silu(x, scale, shift):
        h = x * scale + shift
        return h + h * jnp.tanh(h)

    def put_row(dst, r, src, i, p):
        for ct in range(5):
            lanes = pl.ds(ct * 128, 128)
            x = src[i, :, lanes].astype(F32)
            cut = slice(ct * 128, ct * 128 + 128)
            sd, td = scale_d[p, :, lanes], shift_d[p, :, lanes]
            sl, tl = scale_l[:, cut], shift_l[:, cut]
            for s in range(4):
                piece = x[8 * s : 8 * s + 8]
                act_d[ct, r, pl.ds(8 + 8 * s, 8), :] = silu(piece, sd, td)
                act_l[ct, r, pl.ds(8 + 8 * s, 8), :] = silu(piece, sl, tl)

    @pl.loop(0, ROWS // 4)
    def _(k):
        for p in range(4):
            put_row(None, 4 * k + p + 4, lat, 4 * k + p, p)

    for src, base, ok in ((top, 0, has_up), (bot, ROWS + 4, has_dn)):
        @pl.when(ok)
        def _():
            for p in range(4):
                put_row(None, base + p, src, p, p)

        @pl.when(jnp.logical_not(ok))
        def _():
            for p in range(4):
                for ct in range(5):
                    act_d[ct, base + p] = jnp.zeros((48, 128), F32)
                    act_l[ct, base + p] = jnp.zeros((48, 128), F32)

    for src, at, ok in ((left, 4, has_lf), (right, 40, has_rt)):
        for k0, k1, okr in ((0, 1, has_up), (1, 13, None), (13, 14, has_dn)):
            good = ok if okr is None else ok & okr

            @pl.when(good)
            def _():
                @pl.loop(k0, k1)
                def _(k):
                    for ct in range(5):
                        lanes = pl.ds(ct * 128, 128)
                        cut = slice(ct * 128, ct * 128 + 128)
                        x = src[k, :, lanes].astype(F32)
                        vd = silu(x, scale_e[:, lanes], shift_e[:, lanes])
                        vl = silu(x, scale_l[0:1, cut], shift_l[0:1, cut])
                        for p in range(4):
                            act_d[ct, 4 * k + p, pl.ds(at, 4), :] = vd[4 * p : 4 * p + 4]
                            act_l[ct, 4 * k + p, pl.ds(at, 4), :] = vl[4 * p : 4 * p + 4]

            @pl.when(jnp.logical_not(good))
            def _():
                @pl.loop(k0, k1)
                def _(k):
                    for ct in range(5):
                        for p in range(4):
                            act_d[ct, 4 * k + p, pl.ds(at, 4), :] = jnp.zeros((4, 128), F32)
                            act_l[ct, 4 * k + p, pl.ds(at, 4), :] = jnp.zeros((4, 128), F32)

    mixes = ((0, 2, -1), (1, 2, 1), (2, 1, -1), (1, 3, -1))
    for act, planes, total, bias, near, shifts in (
        (act_d, wd, sum_d, bia_d, 4, (4, 8, 12)),
        (act_l, wl, sum_l, bia_l, 1, (7, 8, 9)),
    ):
        for k in range(4):
            i, j, sign = mixes[k]

            @pl.loop(0, PAIRS)
            def _(t):
                if near == 4:
                    base = 8 * (t // 4) + t % 4
                else:
                    base = 2 * t + 3
                at = pl.ds(pl.multiple_of(t * COLS, COLS), COLS)
                for b in range(3):
                    for ct in range(5):
                        one = act[ct, base + near * i, pl.ds(shifts[b], COLS), :]
                        two = act[ct, base + near * j, pl.ds(shifts[b], COLS), :]
                        mixed = one + two if sign > 0 else one - two
                        lhs[at, pl.ds(b * CH + ct * 128, 128)] = mixed.astype(BF16)

            for n, width in ((0, 256), (256, 256), (512, 128)):
                at = pl.ds(n, width)
                m = jnp.dot(lhs[...], planes[k, :, at], preferred_element_type=F32)
                if k == 0:
                    total[0, :, at] = m + bias[:, at]
                elif k == 1:
                    total[0, :, at] += m
                    total[1, :, at] = m + bias[:, at]
                elif k == 2:
                    total[0, :, at] += m
                    total[1, :, at] -= m
                else:
                    total[1, :, at] -= m

    @pl.loop(0, ROWS // 8)
    def _(u):
        for h in range(2):
            for p in range(4):
                r = 8 * u + 4 * h + p
                from_d = pl.ds(pl.multiple_of((4 * u + p) * COLS, COLS), COLS)
                from_l = pl.ds(pl.multiple_of((4 * u + 2 * h + p // 2) * COLS, COLS), COLS)
                w = wgt[pl.ds(pl.multiple_of(r * COLS, COLS), COLS), :]
                for ct in range(5):
                    lanes = pl.ds(ct * 128, 128)
                    dil = sum_d[h, from_d, lanes].astype(BF16).astype(F32)
                    loc = sum_l[p % 2, from_l, lanes]
                    out[r, :, lanes] = (w * loc + (1.0 - w) * dil).astype(BF16)


VM = pl.BlockSpec(memory_space=pltpu.VMEM)
ANY = pl.BlockSpec(memory_space=pl.ANY)


def per_device(
    latent, blend, gamma_local, beta_local, kernel_local, bias_local,
    gamma_dilated, beta_dilated, kernel_dilated, bias_dilated,
):
    kl = kernel_local.reshape(3, KDIM, CH)
    kd = kernel_dilated.reshape(3, KDIM, CH)
    dma = pltpu.SemaphoreType.DMA
    gathered = pl.pallas_call(
        gather_kernel,
        out_shape=(
            pltpu.VMEM((ROWS, COLS, CH), BF16),
            pltpu.VMEM((4, COLS, CH), BF16),
            pltpu.VMEM((4, COLS, CH), BF16),
            pltpu.VMEM((ROWS // 4 + 2, 16, CH), BF16),
            pltpu.VMEM((ROWS // 4 + 2, 16, CH), BF16),
            pltpu.VMEM((32, 128), F32),
            pltpu.VMEM((4, KDIM, CH), BF16),
            pltpu.VMEM((4, KDIM, CH), BF16),
            pltpu.VMEM((ROWS * COLS, 128), F32),
        ),
        in_specs=[ANY, ANY, ANY, VM],
        out_specs=(VM,) * 9,
        scratch_shapes=[
            pltpu.VMEM((KDIM, CH), BF16),
            pltpu.VMEM((KDIM, CH), BF16),
            pltpu.VMEM((ROWS // 4, 16, CH), BF16),
            pltpu.VMEM((ROWS // 4, 16, CH), BF16),
            pltpu.VMEM((8, 128), F32),
            pltpu.VMEM((8, 128), F32),
            pltpu.VMEM((NROW, 8, 128), F32),
            pltpu.VMEM((NCOL, 8, 128), F32),
            dma, dma((6,)), dma((8,)), dma((8,)),
            dma((NROW,)), dma((NROW,)), dma((NCOL,)), dma((NCOL,)),
        ],
        compiler_params=pltpu.CompilerParams(
            collective_id=0, has_side_effects=True, vmem_limit_bytes=10 * 2**20
        ),
        name="gather",
    )(latent, kl, kd, blend)
    gathered = [pltpu.with_memory_space_constraint(a, pltpu.VMEM) for a in gathered]
    small = [
        a.reshape(1, CH)
        for a in (gamma_local, beta_local, bias_local, gamma_dilated, beta_dilated, bias_dilated)
    ]
    return pl.pallas_call(
        conv_kernel,
        out_shape=jax.ShapeDtypeStruct((ROWS, COLS, CH), BF16),
        in_specs=[VM] * 15,
        out_specs=VM,
        scratch_shapes=[
            pltpu.VMEM((5, 56, 48, 128), F32),
            pltpu.VMEM((5, 56, 48, 128), F32),
            pltpu.VMEM((PAIRS * COLS, KDIM), BF16),
            pltpu.VMEM((2, PAIRS * COLS, CH), F32),
            pltpu.VMEM((2, PAIRS * COLS, CH), F32),
            pltpu.VMEM((4, 8, CH), F32),
            pltpu.VMEM((4, 8, CH), F32),
            pltpu.VMEM((16, CH), F32),
            pltpu.VMEM((16, CH), F32),
        ],
        compiler_params=pltpu.CompilerParams(vmem_limit_bytes=32 * 2**20),
        name="conv",
    )(*gathered, *small)


def solution(mesh):
    placed = (P("row", "col", None), P("row", "col"), P(), P(), P(), P(), P(), P(), P(), P())
    return jax.shard_map(
        per_device, mesh=mesh, in_specs=placed, out_specs=P("row", "col", None), check_vma=False
    )
```

```python
import jax
import jax.numpy as jnp
from jax import lax
from jax.experimental import pallas as pl
from jax.experimental.pallas import tpu as pltpu
from jax.sharding import PartitionSpec as P

CH = 640
GROUPS = 32
PER_GROUP = 20
ROWS = 48
COLS = 32
PAIRS = ROWS // 2
KDIM = 3 * CH
F32 = jnp.float32
BF16 = jnp.bfloat16
MESH = pl.DeviceIdType.MESH
NROW = 8
NCOL = 16
UNITS = ROWS // 4
STEPS = COLS // 4
LOCAL_COUNT = float(UNITS * STEPS * PER_GROUP)


def groups_to_lanes(first_lane):
    chan = lax.broadcasted_iota(jnp.int32, (CH, 128), 0)
    lane = lax.broadcasted_iota(jnp.int32, (CH, 128), 1) - first_lane
    first = lane * PER_GROUP
    inside = (lane >= 0) & (chan >= first) & (chan < first + PER_GROUP)
    return jnp.where(inside, 1.0, 0.0).astype(F32)


def lanes_to_channels():
    lane = lax.broadcasted_iota(jnp.int32, (128, CH), 0)
    chan = lax.broadcasted_iota(jnp.int32, (128, CH), 1)
    first = lane * PER_GROUP
    return jnp.where((chan >= first) & (chan < first + PER_GROUP), 1.0, 0.0).astype(F32)


def exact_dot(a, b):
    return lax.dot_general(
        a, b, (((1,), (0,)), ((), ())), precision=lax.Precision.HIGHEST, preferred_element_type=F32
    )


def merge(tiles, count):
    number = len(tiles)
    total = tiles[0]
    for tile in tiles[1:]:
        total = total + tile
    average = total * (1.0 / number)
    spread = None
    for tile in tiles:
        gap = tile - average
        spread = gap * gap if spread is None else spread + gap * gap
    lanes = lax.broadcasted_iota(jnp.int32, (16, 128), 1)
    return jnp.where(lanes < GROUPS, average, total + count * pltpu.roll(spread, GROUPS, 1))


def gather_kernel(
    lat_hbm, kl_hbm, kd_hbm, blend_hbm,
    xd, xn, stats, wl, wd, wgt,
    lat, blend_ref, mid_l, mid_d, tile1, tile2, got1, got2,
    sem_in, sem_b, sem_w, send_h, recv_h, send1, recv1, send2, recv2,
):
    row = lax.axis_index("row")
    col = lax.axis_index("col")
    has_up = row > 0
    has_dn = row < NROW - 1
    has_lf = col > 0
    has_rt = col < NCOL - 1

    load = pltpu.make_async_copy(lat_hbm, lat, sem_in)
    load.start()
    load_blend = pltpu.make_async_copy(blend_hbm, blend_ref, sem_b)
    load_blend.start()
    weights = []
    for n, (src, planes, mid) in enumerate(((kd_hbm, wd, mid_d), (kl_hbm, wl, mid_l))):
        for m, (a, dst) in enumerate(((0, planes.at[0]), (1, mid), (2, planes.at[3]))):
            copy = pltpu.make_async_copy(src.at[a], dst, sem_w.at[3 * n + m])
            copy.start()
            weights.append(copy)

    barrier = pltpu.get_barrier_semaphore()
    for d in range(1, NROW):
        pl.semaphore_signal(barrier, 1, device_id=(lax.rem(row + d, NROW), col), device_id_type=MESH)
    for d in range(1, NCOL):
        pl.semaphore_signal(barrier, 1, device_id=(row, lax.rem(col + d, NCOL)), device_id_type=MESH)
    for dr, okr in ((-1, has_up), (1, has_dn)):
        for dc, okc in ((-1, has_lf), (1, has_rt)):
            @pl.when(okr & okc)
            def _():
                pl.semaphore_signal(barrier, 1, device_id=(row + dr, col + dc), device_id_type=MESH)

    load.wait()

    def arrange(u, acc):
        rows = []
        for p in range(4):
            x = lat[4 * u + p].astype(F32)
            for ct in range(5):
                xn[ct, 4 * u + p + 1, pl.ds(8, COLS), :] = x[:, ct * 128 : ct * 128 + 128]
            rows.append(x)
        for j in range(STEPS):
            cells = jnp.concatenate([x[4 * j : 4 * j + 4] for x in rows], axis=0)
            acc = acc + cells
            xd[u + 1, j + 1] = cells.astype(BF16)
        return acc

    acc = lax.fori_loop(0, UNITS, arrange, jnp.zeros((16, CH), F32))
    mean = exact_dot(acc, groups_to_lanes(0)) * (1.0 / LOCAL_COUNT)
    centre = exact_dot(mean, lanes_to_channels())

    def squares(u, acc):
        for j in range(STEPS):
            gap = xd[u + 1, j + 1].astype(F32) - centre
            acc = acc + gap * gap
        return acc

    acc = lax.fori_loop(0, UNITS, squares, jnp.zeros((16, CH), F32))
    square = exact_dot(acc, groups_to_lanes(GROUPS))
    lanes = lax.broadcasted_iota(jnp.int32, (16, 128), 1)
    tile1[...] = jnp.where(lanes < GROUPS, mean, square)

    diagonals = (jnp.where(has_up, 1, 0) + jnp.where(has_dn, 1, 0)) * (
        jnp.where(has_lf, 1, 0) + jnp.where(has_rt, 1, 0)
    )
    pl.semaphore_wait(barrier, NROW - 1 + NCOL - 1 + diagonals)

    first = []
    for d in range(1, NROW):
        copy = pltpu.make_async_remote_copy(
            src_ref=tile1, dst_ref=got1.at[d], send_sem=send1.at[d], recv_sem=recv1.at[d],
            device_id=(lax.rem(row + d, NROW), col), device_id_type=MESH,
        )
        copy.start()
        first.append(copy)

    halos = []
    inner_u, inner_j = pl.ds(1, UNITS), pl.ds(1, STEPS)
    for n, (src, dst, dr, dc, ok, got) in enumerate((
        (xd.at[inner_u, STEPS], xd.at[inner_u, 0], 0, 1, has_rt, has_lf),
        (xd.at[inner_u, 1], xd.at[inner_u, STEPS + 1], 0, -1, has_lf, has_rt),
        (xd.at[UNITS, inner_j], xd.at[0, inner_j], 1, 0, has_dn, has_up),
        (xd.at[1, inner_j], xd.at[UNITS + 1, inner_j], -1, 0, has_up, has_dn),
        (xd.at[UNITS, STEPS], xd.at[0, 0], 1, 1, has_dn & has_rt, has_up & has_lf),
        (xd.at[1, STEPS], xd.at[UNITS + 1, 0], -1, 1, has_up & has_rt, has_dn & has_lf),
        (xd.at[UNITS, 1], xd.at[0, STEPS + 1], 1, -1, has_dn & has_lf, has_up & has_rt),
        (xd.at[1, 1], xd.at[UNITS + 1, STEPS + 1], -1, -1, has_up & has_lf, has_dn & has_rt),
    )):
        copy = pltpu.make_async_remote_copy(
            src_ref=src, dst_ref=dst, send_sem=send_h.at[n], recv_sem=recv_h.at[n],
            device_id=(row + dr, col + dc), device_id_type=MESH,
        )
        halos.append((copy, ok, got))
        @pl.when(ok)
        def _():
            copy.start()

    def planes(dst, mid):
        @pl.loop(0, KDIM // 32)
        def _(i):
            at = pl.ds(pl.multiple_of(i * 32, 32), 32)
            ends = dst[0, at, :].astype(F32) + dst[3, at, :].astype(F32)
            centre_tap = mid[at, :].astype(F32)
            dst[1, at, :] = ((ends + centre_tap) * 0.5).astype(BF16)
            dst[2, at, :] = ((ends - centre_tap) * 0.5).astype(BF16)

    load_blend.wait()
    turned = blend_ref[...].astype(F32) * 0.25
    for r in range(ROWS):
        wgt[pl.ds(r * COLS, COLS), :] = jnp.broadcast_to(turned[:, r : r + 1], (COLS, 128))

    for copy in first:
        copy.wait_recv()
    tile2[...] = merge([tile1[...]] + [got1[d] for d in range(1, NROW)], LOCAL_COUNT)
    second = []
    for d in range(1, NCOL):
        copy = pltpu.make_async_remote_copy(
            src_ref=tile2, dst_ref=got2.at[d], send_sem=send2.at[d], recv_sem=recv2.at[d],
            device_id=(row, lax.rem(col + d, NCOL)), device_id_type=MESH,
        )
        copy.start()
        second.append(copy)

    for copy in weights[:3]:
        copy.wait()
    planes(wd, mid_d)
    for copy in weights[3:]:
        copy.wait()
    planes(wl, mid_l)

    for copy, ok, got in halos:
        @pl.when(got)
        def _():
            copy.wait_recv()

        @pl.when(ok)
        def _():
            copy.wait_send()

    for src, at in ((0, 0), (UNITS + 1, ROWS + 1)):
        part = 12 if src == 0 else 0
        for j in range(STEPS):
            x = xd[src, j + 1].astype(F32)[part : part + 4]
            for ct in range(5):
                xn[ct, at, pl.ds(8 + 4 * j, 4), :] = x[:, ct * 128 : ct * 128 + 128]
    for j, q, at in ((0, 3, 7), (STEPS + 1, 0, 8 + COLS)):
        @pl.loop(0, UNITS)
        def _(u):
            x = xd[u + 1, j].astype(F32)
            for p in range(4):
                for ct in range(5):
                    cell = x[4 * p + q : 4 * p + q + 1, ct * 128 : ct * 128 + 128]
                    xn[ct, 4 * u + p + 1, pl.ds(at, 1), :] = cell
        for src, p, r in ((0, 3, 0), (UNITS + 1, 0, ROWS + 1)):
            x = xd[src, j].astype(F32)
            for ct in range(5):
                cell = x[4 * p + q : 4 * p + q + 1, ct * 128 : ct * 128 + 128]
                xn[ct, r, pl.ds(at, 1), :] = cell

    for copy in second:
        copy.wait_recv()
    count = LOCAL_COUNT * NROW
    tile = merge([tile2[...]] + [got2[d] for d in range(1, NCOL)], count)
    count = count * NCOL
    square = pltpu.roll(tile, 128 - GROUPS, 1)

    def everywhere(v):
        return jnp.broadcast_to(jnp.sum(v, axis=0, keepdims=True), (8, 128)) * (1.0 / 16.0)

    var = jnp.where(lanes < GROUPS, square * (1.0 / count), 0.0)
    tile = jnp.where(lanes < GROUPS, tile, 0.0)
    mean_all = everywhere(tile)
    gap = tile - mean_all[0:1]
    stats[pl.ds(0, 16)] = tile
    stats[pl.ds(16, 16)] = lax.rsqrt(var + 1e-05)
    stats[pl.ds(32, 8)] = mean_all
    stats[pl.ds(40, 8)] = lax.rsqrt(everywhere(var + gap * gap) + 1e-05)

    for copy in first + second:
        copy.wait_send()


def conv_kernel(
    xd, xn, stats, wl, wd, wgt,
    gam_l, bet_l, bia_l, gam_d, bet_d, bia_d,
    out,
    lhs_d, even, odd, sum_d, sum_l, turn, scale_d, shift_d, scale_l, shift_l,
):
    row = lax.axis_index("row")
    col = lax.axis_index("col")
    has_up = row > 0
    has_dn = row < NROW - 1
    has_lf = col > 0
    has_rt = col < NCOL - 1

    spread = exact_dot(stats[...], lanes_to_channels())
    for n, gam, bet, scale, shift in (
        (0, gam_d, bet_d, scale_d, shift_d), (32, gam_l, bet_l, scale_l, shift_l)
    ):
        rows = 16 if n == 0 else 8
        by = spread[n + rows : n + 2 * rows] * (gam[...].reshape(1, CH) * 0.5)
        scale[...] = by
        shift[...] = bet[...].reshape(1, CH) * 0.5 - spread[n : n + rows] * by

    def silu(x, scale, shift):
        h = x * scale + shift
        return h + h * jnp.tanh(h)

    def mix(d0, d1, d2, d3):
        return (d0 - d2, d1 + d2, d2 - d1, d1 - d3)

    @pl.loop(0, STEPS + 2)
    def _(j):
        for ct in range(5):
            lanes = pl.ds(ct * 128, 128)
            by, plus = scale_d[:, lanes], shift_d[:, lanes]

            def unit(u):
                return silu(xd[u, j, :, lanes].astype(F32), by, plus)

            d0 = jnp.where(has_up, unit(0), 0.0)
            d1 = unit(1)
            for n in range(UNITS // 2):
                d2 = unit(2 * n + 2)
                d3 = unit(2 * n + 3)
                if n == UNITS // 2 - 1:
                    d3 = jnp.where(has_dn, d3, 0.0)
                for k, v in enumerate(mix(d0, d1, d2, d3)):
                    lhs_d[k, n, j, :, lanes] = v.astype(BF16)
                d0, d1 = d2, d3

    for j, ok in ((0, has_lf), (STEPS + 1, has_rt)):
        @pl.when(jnp.logical_not(ok))
        def _():
            for k in range(4):
                for n in range(UNITS // 2):
                    lhs_d[k, n, j] = jnp.zeros((16, CH), BF16)

    sub = lax.broadcasted_iota(jnp.int32, (8, 128), 0)
    keep_lf = (sub > 0) | has_lf
    keep_rt = (sub < 7) | has_rt
    for ct in range(5):
        lanes = pl.ds(ct * 128, 128)
        by, plus = scale_l[:, lanes], shift_l[:, lanes]

        def line(r):
            cells = [silu(xn[ct, r, pl.ds(7 + m, 8, stride=4), :], by, plus) for m in range(6)]
            cells[0] = jnp.where(keep_lf, cells[0], 0.0)
            cells[5] = jnp.where(keep_rt, cells[5], 0.0)
            return cells

        def pair(t, carry):
            d0, d1 = carry[:6], carry[6:]
            d2 = line(2 * t + 2)
            keep = (t < PAIRS - 1) | has_dn
            d3 = [jnp.where(keep, v, 0.0) for v in line(2 * t + 3)]
            mixed = [mix(*quad) for quad in zip(d0, d1, d2, d3)]
            for k in range(4):
                for half in range(3):
                    v = jnp.concatenate([mixed[2 * half][k], mixed[2 * half + 1][k]], axis=0)
                    even[k, t, pl.ds(16 * half, 16), lanes] = v.astype(BF16)
                for half in range(2):
                    v = jnp.concatenate([mixed[2 * half + 1][k], mixed[2 * half + 2][k]], axis=0)
                    odd[k, t, pl.ds(16 * half, 16), lanes] = v.astype(BF16)
            return tuple(d2) + tuple(d3)

        start = tuple(jnp.where(has_up, v, 0.0) for v in line(0)) + tuple(line(1))
        lax.fori_loop(0, PAIRS, pair, start)

    size = PAIRS * COLS

    def products(get, planes, bias, total, n, width):
        at = pl.ds(n, width)
        for k in range(4):
            m = jnp.dot(get(k), planes[k, :, at], preferred_element_type=F32)
            for c in range(width // 128):
                ct = n // 128 + c
                v = m[:, c * 128 : c * 128 + 128]
                if k == 0:
                    total[0, ct] = v + bias[pl.ds(ct * 128, 128)].reshape(1, 128)
                elif k == 1:
                    total[0, ct] += v
                    total[1, ct] = v + bias[pl.ds(ct * 128, 128)].reshape(1, 128)
                elif k == 2:
                    total[0, ct] += v
                    total[1, ct] -= v
                else:
                    total[1, ct] -= v

    def dilated_lhs(k):
        return jnp.concatenate(
            [lhs_d[k, :, b : b + STEPS].reshape(size, CH) for b in range(3)], axis=1
        )

    def local_lhs(k):
        return jnp.concatenate(
            [
                even[k, :, 0:32].reshape(size, CH),
                odd[k].reshape(size, CH),
                even[k, :, 16:48].reshape(size, CH),
            ],
            axis=1,
        )

    chunks = ((0, 256), (256, 256), (512, 128))
    for n, width in chunks:
        products(dilated_lhs, wd, bia_d, sum_d, n, width)
    lower = sub < 4
    for n, width in chunks:
        products(local_lhs, wl, bia_l, sum_l, n, width)

        @pl.loop(0, UNITS // 2)
        def _(g):
            for h in range(2):
                for c in range(width // 128):
                    ct = n // 128 + c
                    lanes = pl.ds(ct * 128, 128)
                    for p in range(4):
                        at = (4 * g + 2 * h + p // 2) * COLS
                        for m in range(4):
                            cells = pl.ds(pl.multiple_of(at + 8 * m, 8), 8)
                            turn[p, pl.ds(m, 8, stride=4), :] = sum_l[p % 2, ct, cells, :]
                    for e in range(2):
                        parts = []
                        for j in range(STEPS):
                            cells = pl.ds(pl.multiple_of((g * STEPS + j) * 16 + 8 * e, 8), 8)
                            parts.append(sum_d[h, ct, cells, :].astype(BF16).astype(F32))
                        for f in range(2):
                            p = 2 * e + f
                            r = 8 * g + 4 * h + p
                            line = []
                            for v in range(4):
                                a, b = parts[2 * v], parts[2 * v + 1]
                                if f == 0:
                                    line.append(jnp.where(lower, a, pltpu.roll(b, 4, 0)))
                                else:
                                    line.append(jnp.where(lower, pltpu.roll(a, 4, 0), b))
                            dil = jnp.concatenate(line, axis=0)
                            w = wgt[pl.ds(pl.multiple_of(r * COLS, COLS), COLS), :]
                            mixed = w * turn[p] + (1.0 - w) * dil
                            out[r, :, lanes] = mixed.astype(BF16)


VM = pl.BlockSpec(memory_space=pltpu.VMEM)
HB = pl.BlockSpec(memory_space=pltpu.HBM)


def per_device(
    latent, blend, gamma_local, beta_local, kernel_local, bias_local,
    gamma_dilated, beta_dilated, kernel_dilated, bias_dilated,
):
    kl = pltpu.with_memory_space_constraint(kernel_local.reshape(3, KDIM, CH), pltpu.HBM)
    kd = pltpu.with_memory_space_constraint(kernel_dilated.reshape(3, KDIM, CH), pltpu.HBM)
    latent = pltpu.with_memory_space_constraint(latent, pltpu.HBM)
    blend = pltpu.with_memory_space_constraint(blend.T, pltpu.HBM)
    dma = pltpu.SemaphoreType.DMA
    gathered = pl.pallas_call(
        gather_kernel,
        out_shape=(
            pltpu.VMEM((UNITS + 2, STEPS + 2, 16, CH), BF16),
            pltpu.VMEM((5, ROWS + 2, 48, 128), F32),
            pltpu.VMEM((48, 128), F32),
            pltpu.VMEM((4, KDIM, CH), BF16),
            pltpu.VMEM((4, KDIM, CH), BF16),
            pltpu.VMEM((ROWS * COLS, 128), F32),
        ),
        in_specs=[HB, HB, HB, HB],
        out_specs=(VM,) * 6,
        scratch_shapes=[
            pltpu.VMEM((ROWS, COLS, CH), BF16),
            pltpu.VMEM((COLS, ROWS), jnp.int32),
            pltpu.VMEM((KDIM, CH), BF16),
            pltpu.VMEM((KDIM, CH), BF16),
            pltpu.VMEM((16, 128), F32),
            pltpu.VMEM((16, 128), F32),
            pltpu.VMEM((NROW, 16, 128), F32),
            pltpu.VMEM((NCOL, 16, 128), F32),
            dma, dma, dma((6,)), dma((8,)), dma((8,)),
            dma((NROW,)), dma((NROW,)), dma((NCOL,)), dma((NCOL,)),
        ],
        compiler_params=pltpu.CompilerParams(
            collective_id=0, has_side_effects=True, vmem_limit_bytes=12 * 2**20
        ),
        name="gather",
    )(latent, kl, kd, blend)
    gathered = [pltpu.with_memory_space_constraint(a, pltpu.VMEM) for a in gathered]
    small = (gamma_local, beta_local, bias_local, gamma_dilated, beta_dilated, bias_dilated)
    return pl.pallas_call(
        conv_kernel,
        out_shape=jax.ShapeDtypeStruct((ROWS, COLS, CH), BF16),
        in_specs=[VM] * 12,
        out_specs=VM,
        scratch_shapes=[
            pltpu.VMEM((4, UNITS // 2, STEPS + 2, 16, CH), BF16),
            pltpu.VMEM((4, PAIRS, 48, CH), BF16),
            pltpu.VMEM((4, PAIRS, 32, CH), BF16),
            pltpu.VMEM((2, 5, PAIRS * COLS, 128), F32),
            pltpu.VMEM((2, 5, PAIRS * COLS, 128), F32),
            pltpu.VMEM((4, COLS, 128), F32),
            pltpu.VMEM((16, CH), F32),
            pltpu.VMEM((16, CH), F32),
            pltpu.VMEM((8, CH), F32),
            pltpu.VMEM((8, CH), F32),
        ],
        compiler_params=pltpu.CompilerParams(vmem_limit_bytes=30 * 2**20),
        name="conv",
    )(*gathered, *small)


def solution(mesh):
    placed = (P("row", "col", None), P("row", "col"), P(), P(), P(), P(), P(), P(), P(), P())
    return jax.shard_map(
        per_device, mesh=mesh, in_specs=placed, out_specs=P("row", "col", None), check_vma=False
    )
```

```python
import jax
import jax.numpy as jnp
from jax import lax
from jax.experimental import pallas as pl
from jax.experimental.pallas import tpu as pltpu
from jax.sharding import PartitionSpec as P

CH = 640
GROUPS = 32
PER_GROUP = 20
ROWS = 48
COLS = 32
PAIRS = ROWS // 2
KDIM = 3 * CH
F32 = jnp.float32
BF16 = jnp.bfloat16
MESH = pl.DeviceIdType.MESH
NROW = 8
NCOL = 16
UNITS = ROWS // 4
STEPS = COLS // 4
PARTS = 4
LOCAL_COUNT = float(UNITS * STEPS * PER_GROUP)


def groups_to_lanes(first_lane):
    chan = lax.broadcasted_iota(jnp.int32, (CH, 128), 0)
    lane = lax.broadcasted_iota(jnp.int32, (CH, 128), 1) - first_lane
    first = lane * PER_GROUP
    inside = (lane >= 0) & (chan >= first) & (chan < first + PER_GROUP)
    return jnp.where(inside, 1.0, 0.0).astype(F32)


def lanes_to_channels():
    lane = lax.broadcasted_iota(jnp.int32, (128, CH), 0)
    chan = lax.broadcasted_iota(jnp.int32, (128, CH), 1)
    first = lane * PER_GROUP
    return jnp.where((chan >= first) & (chan < first + PER_GROUP), 1.0, 0.0).astype(F32)


def exact_dot(a, b):
    return lax.dot_general(
        a, b, (((1,), (0,)), ((), ())), precision=lax.Precision.HIGHEST, preferred_element_type=F32
    )


def merge(tiles, count):
    number = len(tiles)
    total = tiles[0]
    for tile in tiles[1:]:
        total = total + tile
    average = total * (1.0 / number)
    spread = None
    for tile in tiles:
        gap = tile - average
        spread = gap * gap if spread is None else spread + gap * gap
    lanes = lax.broadcasted_iota(jnp.int32, (16, 128), 1)
    return jnp.where(lanes < GROUPS, average, total + count * pltpu.roll(spread, GROUPS, 1))


def gather_kernel(
    lat_hbm, kl_hbm, kd_hbm, blend_hbm,
    xd, xn, stats, wl, wd, wgt,
    lat, blend_ref, mid_l, mid_d, tile1, tile2, got1, got2,
    sem_in, sem_b, sem_w, send_h, recv_h, send1, recv1, send2, recv2,
):
    row = lax.axis_index("row")
    col = lax.axis_index("col")
    has_up = row > 0
    has_dn = row < NROW - 1
    has_lf = col > 0
    has_rt = col < NCOL - 1

    loads = []
    for n in range(PARTS):
        at = pl.ds(n * (ROWS // PARTS), ROWS // PARTS)
        copy = pltpu.make_async_copy(lat_hbm.at[at], lat.at[at], sem_in.at[n])
        copy.start()
        loads.append(copy)
    load_blend = pltpu.make_async_copy(blend_hbm, blend_ref, sem_b)
    load_blend.start()

    barrier = pltpu.get_barrier_semaphore()
    for d in range(1, NROW):
        pl.semaphore_signal(barrier, 1, device_id=(lax.rem(row + d, NROW), col), device_id_type=MESH)
    for d in range(1, NCOL):
        pl.semaphore_signal(barrier, 1, device_id=(row, lax.rem(col + d, NCOL)), device_id_type=MESH)
    for dr, okr in ((-1, has_up), (1, has_dn)):
        for dc, okc in ((-1, has_lf), (1, has_rt)):
            @pl.when(okr & okc)
            def _():
                pl.semaphore_signal(barrier, 1, device_id=(row + dr, col + dc), device_id_type=MESH)

    loads[0].wait()
    cells = jnp.concatenate([lat[p, 0:16, :].astype(F32)[0:4] for p in range(4)], axis=0)
    centre = jnp.dot(
        cells.astype(BF16), groups_to_lanes(0).astype(BF16), preferred_element_type=F32
    )
    centre = (centre * (1.0 / PER_GROUP)).astype(BF16)
    shift = jnp.dot(centre, lanes_to_channels().astype(BF16), preferred_element_type=F32)

    def arrange(u, carry):
        acc, square = carry
        rows = []
        for p in range(4):
            x = lat[4 * u + p].astype(F32)
            for ct in range(5):
                xn[ct, 4 * u + p + 1, pl.ds(8, COLS), :] = x[:, ct * 128 : ct * 128 + 128]
            rows.append(x)
        for j in range(STEPS):
            cells = jnp.concatenate([x[4 * j : 4 * j + 4] for x in rows], axis=0)
            xd[u + 1, j + 1] = cells.astype(BF16)
            gap = cells - shift
            acc = acc + gap
            square = square + gap * gap
        return acc, square

    carry = (jnp.zeros((16, CH), F32), jnp.zeros((16, CH), F32))
    for n in range(PARTS):
        if n:
            loads[n].wait()
        carry = lax.fori_loop(n * UNITS // PARTS, (n + 1) * UNITS // PARTS, arrange, carry)

    weights = []
    for n, (src, planes, mid) in enumerate(((kd_hbm, wd, mid_d), (kl_hbm, wl, mid_l))):
        for m, (a, dst) in enumerate(((0, planes.at[0]), (1, mid), (2, planes.at[3]))):
            copy = pltpu.make_async_copy(src.at[a], dst, sem_w.at[3 * n + m])
            copy.start()
            weights.append(copy)

    gap = exact_dot(carry[0], groups_to_lanes(0))
    square = exact_dot(carry[1], groups_to_lanes(GROUPS))
    mean = centre.astype(F32) + gap * (1.0 / LOCAL_COUNT)
    square = square - pltpu.roll(gap * gap, GROUPS, 1) * (1.0 / LOCAL_COUNT)
    lanes = lax.broadcasted_iota(jnp.int32, (16, 128), 1)
    tile1[...] = jnp.where(lanes < GROUPS, mean, square)

    diagonals = (jnp.where(has_up, 1, 0) + jnp.where(has_dn, 1, 0)) * (
        jnp.where(has_lf, 1, 0) + jnp.where(has_rt, 1, 0)
    )
    pl.semaphore_wait(barrier, NROW - 1 + NCOL - 1 + diagonals)

    first = []
    for d in range(1, NROW):
        copy = pltpu.make_async_remote_copy(
            src_ref=tile1, dst_ref=got1.at[d], send_sem=send1.at[d], recv_sem=recv1.at[d],
            device_id=(lax.rem(row + d, NROW), col), device_id_type=MESH,
        )
        copy.start()
        first.append(copy)

    halos = []
    inner_u, inner_j = pl.ds(1, UNITS), pl.ds(1, STEPS)
    for n, (src, dst, dr, dc, ok, got) in enumerate((
        (xd.at[inner_u, STEPS], xd.at[inner_u, 0], 0, 1, has_rt, has_lf),
        (xd.at[inner_u, 1], xd.at[inner_u, STEPS + 1], 0, -1, has_lf, has_rt),
        (xd.at[UNITS, inner_j], xd.at[0, inner_j], 1, 0, has_dn, has_up),
        (xd.at[1, inner_j], xd.at[UNITS + 1, inner_j], -1, 0, has_up, has_dn),
        (xd.at[UNITS, STEPS], xd.at[0, 0], 1, 1, has_dn & has_rt, has_up & has_lf),
        (xd.at[1, STEPS], xd.at[UNITS + 1, 0], -1, 1, has_up & has_rt, has_dn & has_lf),
        (xd.at[UNITS, 1], xd.at[0, STEPS + 1], 1, -1, has_dn & has_lf, has_up & has_rt),
        (xd.at[1, 1], xd.at[UNITS + 1, STEPS + 1], -1, -1, has_up & has_lf, has_dn & has_rt),
    )):
        copy = pltpu.make_async_remote_copy(
            src_ref=src, dst_ref=dst, send_sem=send_h.at[n], recv_sem=recv_h.at[n],
            device_id=(row + dr, col + dc), device_id_type=MESH,
        )
        halos.append((copy, ok, got))
        @pl.when(ok)
        def _():
            copy.start()

    def form(dst, mid):
        @pl.loop(0, KDIM // 32)
        def _(i):
            at = pl.ds(pl.multiple_of(i * 32, 32), 32)
            ends = dst[0, at, :].astype(F32) + dst[3, at, :].astype(F32)
            centre_tap = mid[at, :].astype(F32)
            dst[1, at, :] = ((ends + centre_tap) * 0.5).astype(BF16)
            dst[2, at, :] = ((ends - centre_tap) * 0.5).astype(BF16)

    load_blend.wait()
    turned = blend_ref[...].astype(F32) * 0.25
    for r in range(ROWS):
        wgt[pl.ds(r * COLS, COLS), :] = jnp.broadcast_to(turned[:, r : r + 1], (COLS, 128))

    for copy in first:
        copy.wait_recv()
    tile2[...] = merge([tile1[...]] + [got1[d] for d in range(1, NROW)], LOCAL_COUNT)
    second = []
    for d in range(1, NCOL):
        copy = pltpu.make_async_remote_copy(
            src_ref=tile2, dst_ref=got2.at[d], send_sem=send2.at[d], recv_sem=recv2.at[d],
            device_id=(row, lax.rem(col + d, NCOL)), device_id_type=MESH,
        )
        copy.start()
        second.append(copy)

    for copy in weights[:3]:
        copy.wait()
    form(wd, mid_d)
    for copy in weights[3:]:
        copy.wait()
    form(wl, mid_l)

    for copy, ok, got in halos:
        @pl.when(got)
        def _():
            copy.wait_recv()

        @pl.when(ok)
        def _():
            copy.wait_send()

    for src, at in ((0, 0), (UNITS + 1, ROWS + 1)):
        part = 12 if src == 0 else 0
        for j in range(STEPS):
            x = xd[src, j + 1].astype(F32)[part : part + 4]
            for ct in range(5):
                xn[ct, at, pl.ds(8 + 4 * j, 4), :] = x[:, ct * 128 : ct * 128 + 128]
    for j, q, at in ((0, 3, 7), (STEPS + 1, 0, 8 + COLS)):
        @pl.loop(0, UNITS)
        def _(u):
            x = xd[u + 1, j].astype(F32)
            for p in range(4):
                for ct in range(5):
                    cell = x[4 * p + q : 4 * p + q + 1, ct * 128 : ct * 128 + 128]
                    xn[ct, 4 * u + p + 1, pl.ds(at, 1), :] = cell
        for src, p, r in ((0, 3, 0), (UNITS + 1, 0, ROWS + 1)):
            x = xd[src, j].astype(F32)
            for ct in range(5):
                cell = x[4 * p + q : 4 * p + q + 1, ct * 128 : ct * 128 + 128]
                xn[ct, r, pl.ds(at, 1), :] = cell

    for copy in second:
        copy.wait_recv()
    count = LOCAL_COUNT * NROW
    tile = merge([tile2[...]] + [got2[d] for d in range(1, NCOL)], count)
    count = count * NCOL
    square = pltpu.roll(tile, 128 - GROUPS, 1)

    def everywhere(v):
        return jnp.broadcast_to(jnp.sum(v, axis=0, keepdims=True), (8, 128)) * (1.0 / 16.0)

    var = jnp.where(lanes < GROUPS, square * (1.0 / count), 0.0)
    tile = jnp.where(lanes < GROUPS, tile, 0.0)
    mean_all = everywhere(tile)
    gap = tile - mean_all[0:1]
    stats[pl.ds(0, 16)] = tile
    stats[pl.ds(16, 16)] = lax.rsqrt(var + 1e-05)
    stats[pl.ds(32, 8)] = mean_all
    stats[pl.ds(40, 8)] = lax.rsqrt(everywhere(var + gap * gap) + 1e-05)

    for copy in first + second:
        copy.wait_send()


def conv_kernel(
    xd, xn, stats, wl, wd, wgt,
    gam_l, bet_l, bia_l, gam_d, bet_d, bia_d,
    out,
    lhs_d, even, odd, sum_d, total, turn, scale_d, shift_d, scale_l, shift_l,
):
    row = lax.axis_index("row")
    col = lax.axis_index("col")
    has_up = row > 0
    has_dn = row < NROW - 1
    has_lf = col > 0
    has_rt = col < NCOL - 1

    spread = exact_dot(stats[...], lanes_to_channels())
    for n, gam, bet, scale, shift in (
        (0, gam_d, bet_d, scale_d, shift_d), (32, gam_l, bet_l, scale_l, shift_l)
    ):
        rows = 16 if n == 0 else 8
        by = spread[n + rows : n + 2 * rows] * (gam[...].reshape(1, CH) * 0.5)
        scale[...] = by
        shift[...] = bet[...].reshape(1, CH) * 0.5 - spread[n : n + rows] * by

    def silu(x, scale, shift):
        h = x * scale + shift
        return h + h * jnp.tanh(h)

    def mix(d0, d1, d2, d3):
        return (d0 - d2, d1 + d2, d2 - d1, d1 - d3)

    @pl.loop(0, STEPS + 2)
    def _(j):
        for ct in range(5):
            lanes = pl.ds(ct * 128, 128)
            by, plus = scale_d[:, lanes], shift_d[:, lanes]

            def unit(u):
                return silu(xd[u, j, :, lanes].astype(F32), by, plus)

            d0 = jnp.where(has_up, unit(0), 0.0)
            d1 = unit(1)
            for n in range(UNITS // 2):
                d2 = unit(2 * n + 2)
                d3 = unit(2 * n + 3)
                if n == UNITS // 2 - 1:
                    d3 = jnp.where(has_dn, d3, 0.0)
                for k, v in enumerate(mix(d0, d1, d2, d3)):
                    lhs_d[k, n, j, :, lanes] = v.astype(BF16)
                d0, d1 = d2, d3

    for j, ok in ((0, has_lf), (STEPS + 1, has_rt)):
        @pl.when(jnp.logical_not(ok))
        def _():
            for k in range(4):
                for n in range(UNITS // 2):
                    lhs_d[k, n, j] = jnp.zeros((16, CH), BF16)

    sub = lax.broadcasted_iota(jnp.int32, (8, 128), 0)
    keep_lf = (sub > 0) | has_lf
    keep_rt = (sub < 7) | has_rt
    for ct in range(5):
        lanes = pl.ds(ct * 128, 128)
        by, plus = scale_l[:, lanes], shift_l[:, lanes]

        def line(r):
            cells = [silu(xn[ct, r, pl.ds(7 + m, 8, stride=4), :], by, plus) for m in range(6)]
            cells[0] = jnp.where(keep_lf, cells[0], 0.0)
            cells[5] = jnp.where(keep_rt, cells[5], 0.0)
            return cells

        def pair(t, carry):
            d0, d1 = carry[:6], carry[6:]
            d2 = line(2 * t + 2)
            keep = (t < PAIRS - 1) | has_dn
            d3 = [jnp.where(keep, v, 0.0) for v in line(2 * t + 3)]
            mixed = [mix(*quad) for quad in zip(d0, d1, d2, d3)]
            for k in range(4):
                for half in range(3):
                    v = jnp.concatenate([mixed[2 * half][k], mixed[2 * half + 1][k]], axis=0)
                    even[k, t, pl.ds(16 * half, 16), lanes] = v.astype(BF16)
                for half in range(2):
                    v = jnp.concatenate([mixed[2 * half + 1][k], mixed[2 * half + 2][k]], axis=0)
                    odd[k, t, pl.ds(16 * half, 16), lanes] = v.astype(BF16)
            return tuple(d2) + tuple(d3)

        start = tuple(jnp.where(has_up, v, 0.0) for v in line(0)) + tuple(line(1))
        lax.fori_loop(0, PAIRS, pair, start)

    size = PAIRS * COLS

    def products(get, planes, bias, n, width, keep):
        at = pl.ds(n, width)
        for k in range(4):
            m = jnp.dot(get(k), planes[k, :, at], preferred_element_type=F32)
            for c in range(width // 128):
                ct = n // 128 + c
                v = m[:, c * 128 : c * 128 + 128]
                if k == 0:
                    total[0, c] = v + bias[pl.ds(ct * 128, 128)].reshape(1, 128)
                elif k == 1:
                    total[0, c] += v
                    total[1, c] = v + bias[pl.ds(ct * 128, 128)].reshape(1, 128)
                elif k == 2:
                    keep(0, c, ct, total[0, c] + v)
                    total[1, c] -= v
                else:
                    keep(1, c, ct, total[1, c] - v)

    def keep_dilated(h, c, ct, v):
        sum_d[h, ct] = v.astype(BF16)

    def keep_local(h, c, ct, v):
        total[h, c] = v

    def dilated_lhs(k):
        return jnp.concatenate(
            [lhs_d[k, :, b : b + STEPS].reshape(size, CH) for b in range(3)], axis=1
        )

    def local_lhs(k):
        return jnp.concatenate(
            [
                even[k, :, 0:32].reshape(size, CH),
                odd[k].reshape(size, CH),
                even[k, :, 16:48].reshape(size, CH),
            ],
            axis=1,
        )

    chunks = ((0, 512), (512, 128))
    for n, width in chunks:
        products(dilated_lhs, wd, bia_d, n, width, keep_dilated)
    lower = sub < 4
    for n, width in chunks:
        products(local_lhs, wl, bia_l, n, width, keep_local)

        @pl.loop(0, UNITS // 2)
        def _(g):
            for h in range(2):
                for c in range(width // 128):
                    ct = n // 128 + c
                    lanes = pl.ds(ct * 128, 128)
                    for p in range(4):
                        at = (4 * g + 2 * h + p // 2) * COLS
                        for m in range(4):
                            cells = pl.ds(pl.multiple_of(at + 8 * m, 8), 8)
                            turn[p, pl.ds(m, 8, stride=4), :] = total[p % 2, c, cells, :]
                    whole = []
                    for j in range(STEPS):
                        cells = pl.ds(pl.multiple_of((g * STEPS + j) * 16, 16), 16)
                        whole.append(sum_d[h, ct, cells, :].astype(F32))
                    for e in range(2):
                        parts = [x[8 * e : 8 * e + 8] for x in whole]
                        for f in range(2):
                            p = 2 * e + f
                            r = 8 * g + 4 * h + p
                            line = []
                            for v in range(4):
                                a, b = parts[2 * v], parts[2 * v + 1]
                                if f == 0:
                                    line.append(jnp.where(lower, a, pltpu.roll(b, 4, 0)))
                                else:
                                    line.append(jnp.where(lower, pltpu.roll(a, 4, 0), b))
                            dil = jnp.concatenate(line, axis=0)
                            w = wgt[pl.ds(pl.multiple_of(r * COLS, COLS), COLS), :]
                            mixed = w * turn[p] + (1.0 - w) * dil
                            out[r, :, lanes] = mixed.astype(BF16)


VM = pl.BlockSpec(memory_space=pltpu.VMEM)
HB = pl.BlockSpec(memory_space=pltpu.HBM)


def per_device(
    latent, blend, gamma_local, beta_local, kernel_local, bias_local,
    gamma_dilated, beta_dilated, kernel_dilated, bias_dilated,
):
    kl = pltpu.with_memory_space_constraint(kernel_local.reshape(3, KDIM, CH), pltpu.HBM)
    kd = pltpu.with_memory_space_constraint(kernel_dilated.reshape(3, KDIM, CH), pltpu.HBM)
    latent = pltpu.with_memory_space_constraint(latent, pltpu.HBM)
    blend = pltpu.with_memory_space_constraint(blend.T, pltpu.HBM)
    dma = pltpu.SemaphoreType.DMA
    gathered = pl.pallas_call(
        gather_kernel,
        out_shape=(
            pltpu.VMEM((UNITS + 2, STEPS + 2, 16, CH), BF16),
            pltpu.VMEM((5, ROWS + 2, 48, 128), F32),
            pltpu.VMEM((48, 128), F32),
            pltpu.VMEM((4, KDIM, CH), BF16),
            pltpu.VMEM((4, KDIM, CH), BF16),
            pltpu.VMEM((ROWS * COLS, 128), F32),
        ),
        in_specs=[HB, HB, HB, HB],
        out_specs=(VM,) * 6,
        scratch_shapes=[
            pltpu.VMEM((ROWS, COLS, CH), BF16),
            pltpu.VMEM((COLS, ROWS), jnp.int32),
            pltpu.VMEM((KDIM, CH), BF16),
            pltpu.VMEM((KDIM, CH), BF16),
            pltpu.VMEM((16, 128), F32),
            pltpu.VMEM((16, 128), F32),
            pltpu.VMEM((NROW, 16, 128), F32),
            pltpu.VMEM((NCOL, 16, 128), F32),
            dma((PARTS,)), dma, dma((6,)), dma((8,)), dma((8,)),
            dma((NROW,)), dma((NROW,)), dma((NCOL,)), dma((NCOL,)),
        ],
        compiler_params=pltpu.CompilerParams(
            collective_id=0, has_side_effects=True, vmem_limit_bytes=12 * 2**20
        ),
        name="gather",
    )(latent, kl, kd, blend)
    gathered = [pltpu.with_memory_space_constraint(a, pltpu.VMEM) for a in gathered]
    small = (gamma_local, beta_local, bias_local, gamma_dilated, beta_dilated, bias_dilated)
    return pl.pallas_call(
        conv_kernel,
        out_shape=jax.ShapeDtypeStruct((ROWS, COLS, CH), BF16),
        in_specs=[VM] * 12,
        out_specs=VM,
        scratch_shapes=[
            pltpu.VMEM((4, UNITS // 2, STEPS + 2, 16, CH), BF16),
            pltpu.VMEM((4, PAIRS, 48, CH), BF16),
            pltpu.VMEM((4, PAIRS, 32, CH), BF16),
            pltpu.VMEM((2, 5, PAIRS * COLS, 128), BF16),
            pltpu.VMEM((2, 4, PAIRS * COLS, 128), F32),
            pltpu.VMEM((4, COLS, 128), F32),
            pltpu.VMEM((16, CH), F32),
            pltpu.VMEM((16, CH), F32),
            pltpu.VMEM((8, CH), F32),
            pltpu.VMEM((8, CH), F32),
        ],
        compiler_params=pltpu.CompilerParams(vmem_limit_bytes=25 * 2**20),
        name="conv",
    )(*gathered, *small)


def solution(mesh):
    placed = (P("row", "col", None), P("row", "col"), P(), P(), P(), P(), P(), P(), P(), P())
    return jax.shard_map(
        per_device, mesh=mesh, in_specs=placed, out_specs=P("row", "col", None), check_vma=False
    )
```

```python
import jax
import jax.numpy as jnp
from jax import lax
from jax.experimental import pallas as pl
from jax.experimental.pallas import tpu as pltpu
from jax.sharding import PartitionSpec as P

CH = 640
GROUPS = 32
PER_GROUP = 20
ROWS = 48
COLS = 32
PAIRS = ROWS // 2
KDIM = 3 * CH
F32 = jnp.float32
BF16 = jnp.bfloat16
MESH = pl.DeviceIdType.MESH
NROW = 8
NCOL = 16
UNITS = ROWS // 4
STEPS = COLS // 4
BLOCKS = (UNITS // 2) * (STEPS + 2)
PARTS = 4
LOCAL_COUNT = float(UNITS * STEPS * PER_GROUP)


def groups_to_lanes(first_lane):
    chan = lax.broadcasted_iota(jnp.int32, (CH, 128), 0)
    lane = lax.broadcasted_iota(jnp.int32, (CH, 128), 1) - first_lane
    first = lane * PER_GROUP
    inside = (lane >= 0) & (chan >= first) & (chan < first + PER_GROUP)
    return jnp.where(inside, 1.0, 0.0).astype(F32)


def lanes_to_channels():
    lane = lax.broadcasted_iota(jnp.int32, (128, CH), 0)
    chan = lax.broadcasted_iota(jnp.int32, (128, CH), 1)
    first = lane * PER_GROUP
    return jnp.where((chan >= first) & (chan < first + PER_GROUP), 1.0, 0.0).astype(F32)


def exact_dot(a, b):
    return lax.dot_general(
        a, b, (((1,), (0,)), ((), ())), precision=lax.Precision.HIGHEST, preferred_element_type=F32
    )


def merge(tiles, count):
    number = len(tiles)
    total = tiles[0]
    for tile in tiles[1:]:
        total = total + tile
    average = total * (1.0 / number)
    spread = None
    for tile in tiles:
        gap = tile - average
        spread = gap * gap if spread is None else spread + gap * gap
    lanes = lax.broadcasted_iota(jnp.int32, (16, 128), 1)
    return jnp.where(lanes < GROUPS, average, total + count * pltpu.roll(spread, GROUPS, 1))


def gather_kernel(
    lat_hbm, kl_hbm, kd_hbm, blend_hbm,
    xd, xn, stats, wl, wd, wgt,
    lat, blend_ref, mid_l, mid_d, tile1, tile2, got1, got2,
    sem_in, sem_b, sem_w, send_h, recv_h, send1, recv1, send2, recv2,
):
    row = lax.axis_index("row")
    col = lax.axis_index("col")
    has_up = row > 0
    has_dn = row < NROW - 1
    has_lf = col > 0
    has_rt = col < NCOL - 1

    loads = []
    for n in range(PARTS):
        at = pl.ds(n * (ROWS // PARTS), ROWS // PARTS)
        copy = pltpu.make_async_copy(lat_hbm.at[at], lat.at[at], sem_in.at[n])
        copy.start()
        loads.append(copy)
    load_blend = pltpu.make_async_copy(blend_hbm, blend_ref, sem_b)
    load_blend.start()

    barrier = pltpu.get_barrier_semaphore()
    for d in range(1, NROW):
        pl.semaphore_signal(barrier, 1, device_id=(lax.rem(row + d, NROW), col), device_id_type=MESH)
    for d in range(1, NCOL):
        pl.semaphore_signal(barrier, 1, device_id=(row, lax.rem(col + d, NCOL)), device_id_type=MESH)
    for dr, okr in ((-1, has_up), (1, has_dn)):
        for dc, okc in ((-1, has_lf), (1, has_rt)):
            @pl.when(okr & okc)
            def _():
                pl.semaphore_signal(barrier, 1, device_id=(row + dr, col + dc), device_id_type=MESH)

    loads[0].wait()
    cells = jnp.concatenate([lat[p, 0:16, :].astype(F32)[0:4] for p in range(4)], axis=0)
    centre = jnp.dot(
        cells.astype(BF16), groups_to_lanes(0).astype(BF16), preferred_element_type=F32
    )
    centre = (centre * (1.0 / PER_GROUP)).astype(BF16)
    shift = jnp.dot(centre, lanes_to_channels().astype(BF16), preferred_element_type=F32)

    def arrange(u, carry):
        acc, square = carry
        rows = []
        for p in range(4):
            x = lat[4 * u + p].astype(F32)
            for ct in range(5):
                xn[ct, 4 * u + p + 1, pl.ds(0, COLS), :] = x[:, ct * 128 : ct * 128 + 128]
            rows.append(x)
        for j in range(STEPS):
            cells = jnp.concatenate([x[4 * j : 4 * j + 4] for x in rows], axis=0)
            xd[u + 1, j + 1] = cells.astype(BF16)
            gap = cells - shift
            acc = acc + gap
            square = square + gap * gap
        return acc, square

    carry = (jnp.zeros((16, CH), F32), jnp.zeros((16, CH), F32))
    for n in range(PARTS):
        if n:
            loads[n].wait()
        carry = lax.fori_loop(n * UNITS // PARTS, (n + 1) * UNITS // PARTS, arrange, carry)

    weights = []
    for n, (src, planes, mid) in enumerate(((kd_hbm, wd, mid_d), (kl_hbm, wl, mid_l))):
        for m, (a, dst) in enumerate(((0, planes.at[0]), (1, mid), (2, planes.at[3]))):
            copy = pltpu.make_async_copy(src.at[a], dst, sem_w.at[3 * n + m])
            copy.start()
            weights.append(copy)

    gap = exact_dot(carry[0], groups_to_lanes(0))
    square = exact_dot(carry[1], groups_to_lanes(GROUPS))
    mean = centre.astype(F32) + gap * (1.0 / LOCAL_COUNT)
    square = square - pltpu.roll(gap * gap, GROUPS, 1) * (1.0 / LOCAL_COUNT)
    lanes = lax.broadcasted_iota(jnp.int32, (16, 128), 1)
    tile1[...] = jnp.where(lanes < GROUPS, mean, square)

    diagonals = (jnp.where(has_up, 1, 0) + jnp.where(has_dn, 1, 0)) * (
        jnp.where(has_lf, 1, 0) + jnp.where(has_rt, 1, 0)
    )
    pl.semaphore_wait(barrier, NROW - 1 + NCOL - 1 + diagonals)

    first = []
    for d in range(1, NROW):
        copy = pltpu.make_async_remote_copy(
            src_ref=tile1, dst_ref=got1.at[d], send_sem=send1.at[d], recv_sem=recv1.at[d],
            device_id=(lax.rem(row + d, NROW), col), device_id_type=MESH,
        )
        copy.start()
        first.append(copy)

    halos = []
    inner_u, inner_j = pl.ds(1, UNITS), pl.ds(1, STEPS)
    for n, (src, dst, dr, dc, ok, got) in enumerate((
        (xd.at[inner_u, STEPS], xd.at[inner_u, 0], 0, 1, has_rt, has_lf),
        (xd.at[inner_u, 1], xd.at[inner_u, STEPS + 1], 0, -1, has_lf, has_rt),
        (xd.at[UNITS, inner_j], xd.at[0, inner_j], 1, 0, has_dn, has_up),
        (xd.at[1, inner_j], xd.at[UNITS + 1, inner_j], -1, 0, has_up, has_dn),
        (xd.at[UNITS, STEPS], xd.at[0, 0], 1, 1, has_dn & has_rt, has_up & has_lf),
        (xd.at[1, STEPS], xd.at[UNITS + 1, 0], -1, 1, has_up & has_rt, has_dn & has_lf),
        (xd.at[UNITS, 1], xd.at[0, STEPS + 1], 1, -1, has_dn & has_lf, has_up & has_rt),
        (xd.at[1, 1], xd.at[UNITS + 1, STEPS + 1], -1, -1, has_up & has_lf, has_dn & has_rt),
    )):
        copy = pltpu.make_async_remote_copy(
            src_ref=src, dst_ref=dst, send_sem=send_h.at[n], recv_sem=recv_h.at[n],
            device_id=(row + dr, col + dc), device_id_type=MESH,
        )
        halos.append((copy, ok, got))
        @pl.when(ok)
        def _():
            copy.start()

    def form(dst, mid):
        @pl.loop(0, KDIM // 32)
        def _(i):
            at = pl.ds(pl.multiple_of(i * 32, 32), 32)
            ends = dst[0, at, :].astype(F32) + dst[3, at, :].astype(F32)
            centre_tap = mid[at, :].astype(F32)
            dst[1, at, :] = ((ends + centre_tap) * 0.5).astype(BF16)
            dst[2, at, :] = ((ends - centre_tap) * 0.5).astype(BF16)

    load_blend.wait()
    turned = blend_ref[...].astype(F32) * 0.25
    for r in range(ROWS):
        wgt[pl.ds(r * COLS, COLS), :] = jnp.broadcast_to(turned[:, r : r + 1], (COLS, 128)).astype(BF16)

    for copy in first:
        copy.wait_recv()
    tile2[...] = merge([tile1[...]] + [got1[d] for d in range(1, NROW)], LOCAL_COUNT)
    second = []
    for d in range(1, NCOL):
        copy = pltpu.make_async_remote_copy(
            src_ref=tile2, dst_ref=got2.at[d], send_sem=send2.at[d], recv_sem=recv2.at[d],
            device_id=(row, lax.rem(col + d, NCOL)), device_id_type=MESH,
        )
        copy.start()
        second.append(copy)

    for copy in weights[:3]:
        copy.wait()
    form(wd, mid_d)
    for copy in weights[3:]:
        copy.wait()
    form(wl, mid_l)

    for copy, ok, got in halos:
        @pl.when(got)
        def _():
            copy.wait_recv()

        @pl.when(ok)
        def _():
            copy.wait_send()

    for src, at in ((0, 0), (UNITS + 1, ROWS + 1)):
        part = 12 if src == 0 else 0
        for j in range(STEPS):
            x = xd[src, j + 1].astype(F32)[part : part + 4]
            for ct in range(5):
                xn[ct, at, pl.ds(4 * j, 4), :] = x[:, ct * 128 : ct * 128 + 128]
    for j, q, at in ((0, 3, COLS + 1), (STEPS + 1, 0, COLS)):
        @pl.loop(0, UNITS)
        def _(u):
            x = xd[u + 1, j].astype(F32)
            for p in range(4):
                for ct in range(5):
                    cell = x[4 * p + q : 4 * p + q + 1, ct * 128 : ct * 128 + 128]
                    xn[ct, 4 * u + p + 1, pl.ds(at, 1), :] = cell
        for src, p, r in ((0, 3, 0), (UNITS + 1, 0, ROWS + 1)):
            x = xd[src, j].astype(F32)
            for ct in range(5):
                cell = x[4 * p + q : 4 * p + q + 1, ct * 128 : ct * 128 + 128]
                xn[ct, r, pl.ds(at, 1), :] = cell

    for copy in second:
        copy.wait_recv()
    count = LOCAL_COUNT * NROW
    tile = merge([tile2[...]] + [got2[d] for d in range(1, NCOL)], count)
    count = count * NCOL
    square = pltpu.roll(tile, 128 - GROUPS, 1)

    def everywhere(v):
        return jnp.broadcast_to(jnp.sum(v, axis=0, keepdims=True), (8, 128)) * (1.0 / 16.0)

    var = jnp.where(lanes < GROUPS, square * (1.0 / count), 0.0)
    tile = jnp.where(lanes < GROUPS, tile, 0.0)
    mean_all = everywhere(tile)
    gap = tile - mean_all[0:1]
    stats[pl.ds(0, 16)] = tile
    stats[pl.ds(16, 16)] = lax.rsqrt(var + 1e-05)
    stats[pl.ds(32, 8)] = mean_all
    stats[pl.ds(40, 8)] = lax.rsqrt(everywhere(var + gap * gap) + 1e-05)

    for copy in first + second:
        copy.wait_send()


def conv_kernel(
    xd, xn, stats, wl, wd, wgt,
    gam_l, bet_l, bia_l, gam_d, bet_d, bia_d,
    out,
    lhs_d, even, odd, sum_d, total_a, total_b, turn, scale_d, shift_d, scale_l, shift_l,
    sem_a, sem_b,
):
    row = lax.axis_index("row")
    col = lax.axis_index("col")
    has_up = row > 0
    has_dn = row < NROW - 1
    has_lf = col > 0
    has_rt = col < NCOL - 1

    spread = exact_dot(stats[...], lanes_to_channels())
    for n, gam, bet, scale, shift in (
        (0, gam_d, bet_d, scale_d, shift_d), (32, gam_l, bet_l, scale_l, shift_l)
    ):
        rows = 16 if n == 0 else 8
        by = spread[n + rows : n + 2 * rows] * (gam[...].reshape(1, CH) * 0.5)
        scale[...] = by
        shift[...] = bet[...].reshape(1, CH) * 0.5 - spread[n : n + rows] * by

    def silu(x, scale, shift):
        h = x * scale + shift
        return h + h * jnp.tanh(h)

    def mix(d0, d1, d2, d3):
        return (d0 - d2, d1 + d2, d2 - d1, d1 - d3)

    @pl.loop(0, STEPS + 2)
    def _(j):
        for ct in range(5):
            lanes = pl.ds(ct * 128, 128)
            by, plus = scale_d[:, lanes], shift_d[:, lanes]

            def unit(u):
                return silu(xd[u, j, :, lanes].astype(F32), by, plus)

            d0 = jnp.where(has_up, unit(0), 0.0)
            d1 = unit(1)
            for n in range(UNITS // 2):
                d2 = unit(2 * n + 2)
                d3 = unit(2 * n + 3)
                if n == UNITS // 2 - 1:
                    d3 = jnp.where(has_dn, d3, 0.0)
                for k, v in enumerate(mix(d0, d1, d2, d3)):
                    lhs_d[k * BLOCKS + n * (STEPS + 2) + j, :, lanes] = v.astype(BF16)
                d0, d1 = d2, d3

    for j, ok in ((0, has_lf), (STEPS + 1, has_rt)):
        @pl.when(jnp.logical_not(ok))
        def _():
            for k in range(4):
                for n in range(UNITS // 2):
                    lhs_d[k * BLOCKS + n * (STEPS + 2) + j] = jnp.zeros((16, CH), BF16)

    sub = lax.broadcasted_iota(jnp.int32, (8, 128), 0)
    first = sub == 0
    keep_rt = (sub < 7) | has_rt

    def form_local(t0, t1):
        for ct in range(5):
            lanes = pl.ds(ct * 128, 128)
            by, plus = scale_l[:, lanes], shift_l[:, lanes]

            def line(r):
                cells = [silu(xn[ct, r, pl.ds(m, 8, stride=4), :], by, plus) for m in range(5)]
                cells[4] = jnp.where(keep_rt, cells[4], 0.0)
                edge = silu(jnp.broadcast_to(xn[ct, r, pl.ds(COLS + 1, 1), :], (8, 128)), by, plus)
                edge = jnp.where(has_lf, edge, 0.0)
                cells.insert(0, jnp.where(first, edge, pltpu.roll(cells[3], 1, 0)))
                if r == 0:
                    cells = [jnp.where(has_up, v, 0.0) for v in cells]
                if r == ROWS + 1:
                    cells = [jnp.where(has_dn, v, 0.0) for v in cells]
                return cells

            d0, d1 = line(2 * t0), line(2 * t0 + 1)
            for t in range(t0, t1):
                d2, d3 = line(2 * t + 2), line(2 * t + 3)
                mixed = [mix(*quad) for quad in zip(d0, d1, d2, d3)]
                for k in range(4):
                    for half in range(3):
                        v = jnp.concatenate([mixed[2 * half][k], mixed[2 * half + 1][k]], axis=0)
                        even[k, t, pl.ds(16 * half, 16), lanes] = v.astype(BF16)
                    for half in range(2):
                        v = jnp.concatenate([mixed[2 * half + 1][k], mixed[2 * half + 2][k]], axis=0)
                        odd[k, t, pl.ds(16 * half, 16), lanes] = v.astype(BF16)
                d0, d1 = d2, d3

    size = PAIRS * COLS

    def products(get, planes, bias, n, width, total, keep, beside=None):
        at = pl.ds(n, width)
        for k in range(4):
            m = jnp.dot(get(k), planes[k, :, at], preferred_element_type=F32)
            if beside is not None:
                beside(k)
            for c in range(width // 128):
                ct = n // 128 + c
                v = m[:, c * 128 : c * 128 + 128]
                if k == 0:
                    total[0, c] = v + bias[pl.ds(ct * 128, 128)].reshape(1, 128)
                elif k == 1:
                    total[0, c] += v
                    total[1, c] = v + bias[pl.ds(ct * 128, 128)].reshape(1, 128)
                elif k == 2:
                    keep(0, c, ct, total[0, c] + v)
                    total[1, c] -= v
                else:
                    keep(1, c, ct, total[1, c] - v)

    def keep_dilated(h, c, ct, v):
        sum_d[h, ct] = v.astype(BF16)

    def keep_local(total):
        def keep(h, c, ct, v):
            total[h, c] = v

        return keep

    def dilated_lhs(k):
        taps = []
        for b in range(3):
            lines = [
                lhs_d[pl.ds(k * BLOCKS + n * (STEPS + 2) + b, STEPS)] for n in range(UNITS // 2)
            ]
            taps.append(jnp.concatenate(lines, axis=0).reshape(size, CH))
        return jnp.concatenate(taps, axis=1)

    def local_lhs(k):
        return jnp.concatenate(
            [
                even[k, :, 0:32].reshape(size, CH),
                odd[k].reshape(size, CH),
                even[k, :, 16:48].reshape(size, CH),
            ],
            axis=1,
        )

    lower = sub < 4

    def blend(total, n, width, g, h):
        for c in range(width // 128):
            ct = n // 128 + c
            lanes = pl.ds(ct * 128, 128)
            for p in range(4):
                at = (4 * g + 2 * h + p // 2) * COLS
                for m in range(4):
                    cells = total[p % 2, c, pl.ds(at + 8 * m, 8), :]
                    turn[c, h, p, pl.ds(m, 8, stride=4), :] = cells
            whole = []
            for j in range(STEPS):
                whole.append(sum_d[h, ct, pl.ds((g * STEPS + j) * 16, 16), :].astype(F32))
            for e in range(2):
                parts = [x[8 * e : 8 * e + 8] for x in whole]
                for f in range(2):
                    p = 2 * e + f
                    r = 8 * g + 4 * h + p
                    line = []
                    for v in range(4):
                        a, b = parts[2 * v], parts[2 * v + 1]
                        if f == 0:
                            line.append(jnp.where(lower, a, pltpu.roll(b, 4, 0)))
                        else:
                            line.append(jnp.where(lower, pltpu.roll(a, 4, 0), b))
                    dil = jnp.concatenate(line, axis=0)
                    w = wgt[pl.ds(r * COLS, COLS), :].astype(F32)
                    mixed = w * turn[c, h, p] + (1.0 - w) * dil
                    mixed = mixed.astype(BF16)
                    lhs_d[2 * r, :, lanes] = mixed[0:16]
                    lhs_d[2 * r + 1, :, lanes] = mixed[16:32]

    quarter = PAIRS // 4
    products(
        dilated_lhs, wd, bia_d, 0, 512, total_a, keep_dilated,
        lambda k: form_local(k * quarter, (k + 1) * quarter),
    )
    products(dilated_lhs, wd, bia_d, 512, 128, total_b, keep_dilated)
    products(local_lhs, wl, bia_l, 0, 512, total_a, keep_local(total_a))

    def beside(k):
        for unit in range(3 * k, 3 * k + 3):
            blend(total_a, 0, 512, unit // 2, unit % 2)

    products(local_lhs, wl, bia_l, 512, 128, total_b, keep_local(total_b), beside)
    result = lhs_d.at[pl.ds(0, 2 * ROWS)]
    store_a = pltpu.make_async_copy(result.at[:, :, pl.ds(0, 512)], out.at[:, :, pl.ds(0, 512)], sem_a)
    store_a.start()
    for unit in range(UNITS):
        blend(total_b, 512, 128, unit // 2, unit % 2)
    store_b = pltpu.make_async_copy(result.at[:, :, pl.ds(512, 128)], out.at[:, :, pl.ds(512, 128)], sem_b)
    store_b.start()
    store_a.wait()
    store_b.wait()


VM = pl.BlockSpec(memory_space=pltpu.VMEM)
HB = pl.BlockSpec(memory_space=pltpu.HBM)


def per_device(
    latent, blend, gamma_local, beta_local, kernel_local, bias_local,
    gamma_dilated, beta_dilated, kernel_dilated, bias_dilated,
):
    kl = pltpu.with_memory_space_constraint(kernel_local.reshape(3, KDIM, CH), pltpu.HBM)
    kd = pltpu.with_memory_space_constraint(kernel_dilated.reshape(3, KDIM, CH), pltpu.HBM)
    latent = pltpu.with_memory_space_constraint(latent, pltpu.HBM)
    blend = pltpu.with_memory_space_constraint(blend.T, pltpu.HBM)
    dma = pltpu.SemaphoreType.DMA
    gathered = pl.pallas_call(
        gather_kernel,
        out_shape=(
            pltpu.VMEM((UNITS + 2, STEPS + 2, 16, CH), BF16),
            pltpu.VMEM((5, ROWS + 2, 40, 128), F32),
            pltpu.VMEM((48, 128), F32),
            pltpu.VMEM((4, KDIM, CH), BF16),
            pltpu.VMEM((4, KDIM, CH), BF16),
            pltpu.VMEM((ROWS * COLS, 128), BF16),
        ),
        in_specs=[HB, HB, HB, HB],
        out_specs=(VM,) * 6,
        scratch_shapes=[
            pltpu.VMEM((ROWS, COLS, CH), BF16),
            pltpu.VMEM((COLS, ROWS), jnp.int32),
            pltpu.VMEM((KDIM, CH), BF16),
            pltpu.VMEM((KDIM, CH), BF16),
            pltpu.VMEM((16, 128), F32),
            pltpu.VMEM((16, 128), F32),
            pltpu.VMEM((NROW, 16, 128), F32),
            pltpu.VMEM((NCOL, 16, 128), F32),
            dma((PARTS,)), dma, dma((6,)), dma((8,)), dma((8,)),
            dma((NROW,)), dma((NROW,)), dma((NCOL,)), dma((NCOL,)),
        ],
        compiler_params=pltpu.CompilerParams(
            collective_id=0, has_side_effects=True, vmem_limit_bytes=12 * 2**20
        ),
        name="gather",
    )(latent, kl, kd, blend)
    gathered = [pltpu.with_memory_space_constraint(a, pltpu.VMEM) for a in gathered]
    small = (gamma_local, beta_local, bias_local, gamma_dilated, beta_dilated, bias_dilated)
    return pl.pallas_call(
        conv_kernel,
        out_shape=jax.ShapeDtypeStruct((2 * ROWS, 16, CH), BF16),
        in_specs=[VM] * 12,
        out_specs=HB,
        scratch_shapes=[
            pltpu.VMEM((4 * BLOCKS, 16, CH), BF16),
            pltpu.VMEM((4, PAIRS, 48, CH), BF16),
            pltpu.VMEM((4, PAIRS, 32, CH), BF16),
            pltpu.VMEM((2, 5, PAIRS * COLS, 128), BF16),
            pltpu.VMEM((2, 4, PAIRS * COLS, 128), F32),
            pltpu.VMEM((2, 1, PAIRS * COLS, 128), F32),
            pltpu.VMEM((4, 2, 4, COLS, 128), F32),
            pltpu.VMEM((16, CH), F32),
            pltpu.VMEM((16, CH), F32),
            pltpu.VMEM((8, CH), F32),
            pltpu.VMEM((8, CH), F32),
            dma,
            dma,
        ],
        compiler_params=pltpu.CompilerParams(vmem_limit_bytes=26 * 2**20 + 2**18),
        name="conv",
    )(*gathered, *small).reshape(ROWS, COLS, CH)


def solution(mesh):
    placed = (P("row", "col", None), P("row", "col"), P(), P(), P(), P(), P(), P(), P(), P())
    return jax.shard_map(
        per_device, mesh=mesh, in_specs=placed, out_specs=P("row", "col", None), check_vma=False
    )
```

```python
import jax
import jax.numpy as jnp
from jax import lax
from jax.experimental import pallas as pl
from jax.experimental.pallas import tpu as pltpu
from jax.sharding import PartitionSpec as P

CH = 640
GROUPS = 32
PER_GROUP = 20
ROWS = 48
COLS = 32
PAIRS = ROWS // 2
KDIM = 3 * CH
F32 = jnp.float32
BF16 = jnp.bfloat16
MESH = pl.DeviceIdType.MESH
NROW = 8
NCOL = 16
UNITS = ROWS // 4
STEPS = COLS // 4
BLOCKS = (UNITS // 2) * (STEPS + 2)
PARTS = 4
LOCAL_COUNT = float(UNITS * STEPS * PER_GROUP)


def groups_to_lanes(first_lane):
    chan = lax.broadcasted_iota(jnp.int32, (CH, 128), 0)
    lane = lax.broadcasted_iota(jnp.int32, (CH, 128), 1) - first_lane
    first = lane * PER_GROUP
    inside = (lane >= 0) & (chan >= first) & (chan < first + PER_GROUP)
    return jnp.where(inside, 1.0, 0.0).astype(F32)


def lanes_to_channels():
    lane = lax.broadcasted_iota(jnp.int32, (128, CH), 0)
    chan = lax.broadcasted_iota(jnp.int32, (128, CH), 1)
    first = lane * PER_GROUP
    return jnp.where((chan >= first) & (chan < first + PER_GROUP), 1.0, 0.0).astype(F32)


def exact_dot(a, b):
    return lax.dot_general(
        a, b, (((1,), (0,)), ((), ())), precision=lax.Precision.HIGHEST, preferred_element_type=F32
    )


def merge(tiles, count):
    number = len(tiles)
    total = tiles[0]
    for tile in tiles[1:]:
        total = total + tile
    average = total * (1.0 / number)
    spread = None
    for tile in tiles:
        gap = tile - average
        spread = gap * gap if spread is None else spread + gap * gap
    lanes = lax.broadcasted_iota(jnp.int32, (8, 128), 1)
    is_mean = (lanes // GROUPS) % 2 == 0
    return jnp.where(is_mean, average, total + count * pltpu.roll(spread, GROUPS, 1))


def gather_kernel(
    lat_hbm, kl_hbm, kd_hbm, blend_hbm,
    xd, xn, stats, wl, wd, wgt,
    lat, blend_ref, mid_l, mid_d, tile1, tile2, got1, got2,
    sem_in, sem_b, sem_w, send_h, recv_h, send1, recv1, send2, recv2,
):
    row = lax.axis_index("row")
    col = lax.axis_index("col")
    has_up = row > 0
    has_dn = row < NROW - 1
    has_lf = col > 0
    has_rt = col < NCOL - 1

    loads = []
    for n in range(PARTS):
        at = pl.ds(n * (ROWS // PARTS), ROWS // PARTS)
        copy = pltpu.make_async_copy(lat_hbm.at[at], lat.at[at], sem_in.at[n])
        copy.start()
        loads.append(copy)
    load_blend = pltpu.make_async_copy(blend_hbm, blend_ref, sem_b)
    load_blend.start()

    barrier = pltpu.get_barrier_semaphore()
    for d in range(1, NROW):
        pl.semaphore_signal(barrier, 1, device_id=(lax.rem(row + d, NROW), col), device_id_type=MESH)
    for d in range(1, NCOL):
        pl.semaphore_signal(barrier, 1, device_id=(row, lax.rem(col + d, NCOL)), device_id_type=MESH)
    for dr, okr in ((-1, has_up), (1, has_dn)):
        for dc, okc in ((-1, has_lf), (1, has_rt)):
            @pl.when(okr & okc)
            def _():
                pl.semaphore_signal(barrier, 1, device_id=(row + dr, col + dc), device_id_type=MESH)

    loads[0].wait()
    cells = jnp.concatenate([lat[p, 0:16, :].astype(F32)[0:4] for p in range(4)], axis=0)
    centre = jnp.dot(
        cells.astype(BF16), groups_to_lanes(0).astype(BF16), preferred_element_type=F32
    )
    centre = (centre * (1.0 / PER_GROUP)).astype(BF16)
    shift = jnp.dot(centre, lanes_to_channels().astype(BF16), preferred_element_type=F32)

    def arrange(u, carry):
        acc, square = carry
        rows = []
        for p in range(4):
            x = lat[4 * u + p].astype(F32)
            for ct in range(5):
                xn[ct, 4 * u + p + 1, pl.ds(0, COLS), :] = x[:, ct * 128 : ct * 128 + 128]
            rows.append(x)
        for j in range(STEPS):
            cells = jnp.concatenate([x[4 * j : 4 * j + 4] for x in rows], axis=0)
            xd[u + 1, j + 1] = cells.astype(BF16)
            gap = cells - shift
            acc = acc + gap
            square = square + gap * gap
        return acc, square

    carry = (jnp.zeros((16, CH), F32), jnp.zeros((16, CH), F32))
    for n in range(PARTS):
        if n:
            loads[n].wait()
        carry = lax.fori_loop(n * UNITS // PARTS, (n + 1) * UNITS // PARTS, arrange, carry)

    weights = []
    for n, (src, planes, mid) in enumerate(((kd_hbm, wd, mid_d), (kl_hbm, wl, mid_l))):
        for m, (a, dst) in enumerate(((0, planes.at[0]), (1, mid), (2, planes.at[3]))):
            copy = pltpu.make_async_copy(src.at[a], dst, sem_w.at[3 * n + m])
            copy.start()
            weights.append(copy)

    gap = exact_dot(carry[0], groups_to_lanes(0))
    square = exact_dot(carry[1], groups_to_lanes(GROUPS))
    mean = centre.astype(F32) + gap * (1.0 / LOCAL_COUNT)
    square = square - pltpu.roll(gap * gap, GROUPS, 1) * (1.0 / LOCAL_COUNT)
    lanes = lax.broadcasted_iota(jnp.int32, (16, 128), 1)
    tile = jnp.where(lanes < GROUPS, mean, jnp.where(lanes < 2 * GROUPS, square, 0.0))
    tile1[...] = tile[0:8] + pltpu.roll(tile[8:16], 2 * GROUPS, 1)

    diagonals = (jnp.where(has_up, 1, 0) + jnp.where(has_dn, 1, 0)) * (
        jnp.where(has_lf, 1, 0) + jnp.where(has_rt, 1, 0)
    )
    pl.semaphore_wait(barrier, NROW - 1 + NCOL - 1 + diagonals)

    first = []
    for d in range(1, NROW):
        copy = pltpu.make_async_remote_copy(
            src_ref=tile1, dst_ref=got1.at[d], send_sem=send1.at[d], recv_sem=recv1.at[d],
            device_id=(lax.rem(row + d, NROW), col), device_id_type=MESH,
        )
        copy.start()
        first.append(copy)

    halos = []
    inner_u, inner_j = pl.ds(1, UNITS), pl.ds(1, STEPS)
    for n, (src, dst, dr, dc, ok, got) in enumerate((
        (xd.at[inner_u, STEPS], xd.at[inner_u, 0], 0, 1, has_rt, has_lf),
        (xd.at[inner_u, 1], xd.at[inner_u, STEPS + 1], 0, -1, has_lf, has_rt),
        (xd.at[UNITS, inner_j], xd.at[0, inner_j], 1, 0, has_dn, has_up),
        (xd.at[1, inner_j], xd.at[UNITS + 1, inner_j], -1, 0, has_up, has_dn),
        (xd.at[UNITS, STEPS], xd.at[0, 0], 1, 1, has_dn & has_rt, has_up & has_lf),
        (xd.at[1, STEPS], xd.at[UNITS + 1, 0], -1, 1, has_up & has_rt, has_dn & has_lf),
        (xd.at[UNITS, 1], xd.at[0, STEPS + 1], 1, -1, has_dn & has_lf, has_up & has_rt),
        (xd.at[1, 1], xd.at[UNITS + 1, STEPS + 1], -1, -1, has_up & has_lf, has_dn & has_rt),
    )):
        copy = pltpu.make_async_remote_copy(
            src_ref=src, dst_ref=dst, send_sem=send_h.at[n], recv_sem=recv_h.at[n],
            device_id=(row + dr, col + dc), device_id_type=MESH,
        )
        halos.append((copy, ok, got))
        @pl.when(ok)
        def _():
            copy.start()

    def form(dst, mid):
        @pl.loop(0, KDIM // 32)
        def _(i):
            at = pl.ds(pl.multiple_of(i * 32, 32), 32)
            ends = dst[0, at, :].astype(F32) + dst[3, at, :].astype(F32)
            centre_tap = mid[at, :].astype(F32)
            dst[1, at, :] = ((ends + centre_tap) * 0.5).astype(BF16)
            dst[2, at, :] = ((ends - centre_tap) * 0.5).astype(BF16)

    load_blend.wait()
    turned = blend_ref[...].astype(F32) * 0.25
    for r in range(ROWS):
        wgt[pl.ds(r * COLS, COLS), :] = jnp.broadcast_to(turned[:, r : r + 1], (COLS, 128)).astype(BF16)

    for copy in first:
        copy.wait_recv()
    tile2[...] = merge([tile1[...]] + [got1[d] for d in range(1, NROW)], LOCAL_COUNT)
    second = []
    for d in range(1, NCOL):
        copy = pltpu.make_async_remote_copy(
            src_ref=tile2, dst_ref=got2.at[d], send_sem=send2.at[d], recv_sem=recv2.at[d],
            device_id=(row, lax.rem(col + d, NCOL)), device_id_type=MESH,
        )
        copy.start()
        second.append(copy)

    for copy in weights[:3]:
        copy.wait()
    form(wd, mid_d)

    for copy in weights[3:]:
        copy.wait()
    form(wl, mid_l)

    for copy, ok, got in halos:
        @pl.when(got)
        def _():
            copy.wait_recv()

        @pl.when(ok)
        def _():
            copy.wait_send()

    for src, at in ((0, 0), (UNITS + 1, ROWS + 1)):
        part = 12 if src == 0 else 0
        for j in range(STEPS):
            x = xd[src, j + 1].astype(F32)[part : part + 4]
            for ct in range(5):
                xn[ct, at, pl.ds(4 * j, 4), :] = x[:, ct * 128 : ct * 128 + 128]
    for j, q, at in ((0, 3, COLS + 1), (STEPS + 1, 0, COLS)):
        @pl.loop(0, UNITS)
        def _(u):
            x = xd[u + 1, j].astype(F32)
            for p in range(4):
                for ct in range(5):
                    cell = x[4 * p + q : 4 * p + q + 1, ct * 128 : ct * 128 + 128]
                    xn[ct, 4 * u + p + 1, pl.ds(at, 1), :] = cell
        for src, p, r in ((0, 3, 0), (UNITS + 1, 0, ROWS + 1)):
            x = xd[src, j].astype(F32)
            for ct in range(5):
                cell = x[4 * p + q : 4 * p + q + 1, ct * 128 : ct * 128 + 128]
                xn[ct, r, pl.ds(at, 1), :] = cell

    for copy in second:
        copy.wait_recv()
    tile = merge([tile2[...]] + [got2[d] for d in range(1, NCOL)], LOCAL_COUNT * NROW)
    tile = jnp.concatenate([tile, pltpu.roll(tile, 2 * GROUPS, 1)], axis=0)
    count = LOCAL_COUNT * NROW * NCOL
    square = pltpu.roll(tile, 128 - GROUPS, 1)

    def everywhere(v):
        return jnp.broadcast_to(jnp.sum(v, axis=0, keepdims=True), (8, 128)) * (1.0 / 16.0)

    var = jnp.where(lanes < GROUPS, square * (1.0 / count), 0.0)
    tile = jnp.where(lanes < GROUPS, tile, 0.0)
    mean_all = everywhere(tile)
    gap = tile - mean_all[0:1]
    stats[pl.ds(0, 16)] = tile
    stats[pl.ds(16, 16)] = lax.rsqrt(var + 1e-05)
    stats[pl.ds(32, 8)] = mean_all
    stats[pl.ds(40, 8)] = lax.rsqrt(everywhere(var + gap * gap) + 1e-05)

    for copy in first + second:
        copy.wait_send()


def conv_kernel(
    xd, xn, stats, wl, wd, wgt,
    gam_l, bet_l, bia_l, gam_d, bet_d, bia_d,
    out,
    lhs_d, even, odd, sum_d, total_a, total_b, turn, scale_d, shift_d, scale_l, shift_l,
    sem_out,
):
    row = lax.axis_index("row")
    col = lax.axis_index("col")
    has_up = row > 0
    has_dn = row < NROW - 1
    has_lf = col > 0
    has_rt = col < NCOL - 1

    spread = exact_dot(stats[...], lanes_to_channels())
    for n, gam, bet, scale, shift in (
        (0, gam_d, bet_d, scale_d, shift_d), (32, gam_l, bet_l, scale_l, shift_l)
    ):
        rows = 16 if n == 0 else 8
        by = spread[n + rows : n + 2 * rows] * (gam[...].reshape(1, CH) * 0.5)
        scale[...] = by
        shift[...] = bet[...].reshape(1, CH) * 0.5 - spread[n : n + rows] * by

    def silu(x, scale, shift):
        h = x * scale + shift
        return h + h * jnp.tanh(h)

    def mix(d0, d1, d2, d3):
        return (d0 - d2, d1 + d2, d2 - d1, d1 - d3)

    @pl.loop(0, STEPS + 2)
    def _(j):
        for ct in range(5):
            lanes = pl.ds(ct * 128, 128)
            by, plus = scale_d[:, lanes], shift_d[:, lanes]

            def unit(u):
                return silu(xd[u, j, :, lanes].astype(F32), by, plus)

            d0 = jnp.where(has_up, unit(0), 0.0)
            d1 = unit(1)
            for n in range(UNITS // 2):
                d2 = unit(2 * n + 2)
                d3 = unit(2 * n + 3)
                if n == UNITS // 2 - 1:
                    d3 = jnp.where(has_dn, d3, 0.0)
                for k, v in enumerate(mix(d0, d1, d2, d3)):
                    lhs_d[k * BLOCKS + n * (STEPS + 2) + j, :, lanes] = v.astype(BF16)
                d0, d1 = d2, d3

    for j, ok in ((0, has_lf), (STEPS + 1, has_rt)):
        @pl.when(jnp.logical_not(ok))
        def _():
            for k in range(4):
                for n in range(UNITS // 2):
                    lhs_d[k * BLOCKS + n * (STEPS + 2) + j] = jnp.zeros((16, CH), BF16)

    sub = lax.broadcasted_iota(jnp.int32, (8, 128), 0)
    first = sub == 0
    keep_rt = (sub < 7) | has_rt

    def form_local(t0, t1):
        for ct in range(5):
            lanes = pl.ds(ct * 128, 128)
            by, plus = scale_l[:, lanes], shift_l[:, lanes]

            def line(r):
                cells = [silu(xn[ct, r, pl.ds(m, 8, stride=4), :], by, plus) for m in range(5)]
                cells[4] = jnp.where(keep_rt, cells[4], 0.0)
                edge = silu(jnp.broadcast_to(xn[ct, r, pl.ds(COLS + 1, 1), :], (8, 128)), by, plus)
                edge = jnp.where(has_lf, edge, 0.0)
                cells.insert(0, jnp.where(first, edge, pltpu.roll(cells[3], 1, 0)))
                if r == 0:
                    cells = [jnp.where(has_up, v, 0.0) for v in cells]
                if r == ROWS + 1:
                    cells = [jnp.where(has_dn, v, 0.0) for v in cells]
                return cells

            d0, d1 = line(2 * t0), line(2 * t0 + 1)
            for t in range(t0, t1):
                d2, d3 = line(2 * t + 2), line(2 * t + 3)
                mixed = [mix(*quad) for quad in zip(d0, d1, d2, d3)]
                for k in range(4):
                    for half in range(3):
                        v = jnp.concatenate([mixed[2 * half][k], mixed[2 * half + 1][k]], axis=0)
                        even[k, t, pl.ds(16 * half, 16), lanes] = v.astype(BF16)
                    for half in range(2):
                        v = jnp.concatenate([mixed[2 * half + 1][k], mixed[2 * half + 2][k]], axis=0)
                        odd[k, t, pl.ds(16 * half, 16), lanes] = v.astype(BF16)
                d0, d1 = d2, d3

    size = PAIRS * COLS

    def products(get, planes, bias, n, width, total, keep, beside=None, after=None):
        at = pl.ds(n, width)
        for k in range(4):
            m = jnp.dot(get(k), planes[k, :, at], preferred_element_type=F32)
            if beside is not None:
                beside(k)
            for c in range(width // 128):
                ct = n // 128 + c
                v = m[:, c * 128 : c * 128 + 128]
                if k == 0:
                    total[0, c] = v + bias[pl.ds(ct * 128, 128)].reshape(1, 128)
                elif k == 1:
                    total[0, c] += v
                    total[1, c] = v + bias[pl.ds(ct * 128, 128)].reshape(1, 128)
                elif k == 2:
                    keep(0, c, ct, total[0, c] + v)
                    total[1, c] -= v
                else:
                    keep(1, c, ct, total[1, c] - v)
            if after is not None:
                after(k)

    def keep_dilated(h, c, ct, v):
        sum_d[h, ct] = v.astype(BF16)

    def keep_local(total):
        def keep(h, c, ct, v):
            total[h, c] = v

        return keep

    def dilated_lhs(k):
        taps = []
        for b in range(3):
            lines = [
                lhs_d[pl.ds(k * BLOCKS + n * (STEPS + 2) + b, STEPS)] for n in range(UNITS // 2)
            ]
            taps.append(jnp.concatenate(lines, axis=0).reshape(size, CH))
        return jnp.concatenate(taps, axis=1)

    def local_lhs(k):
        return jnp.concatenate(
            [
                even[k, :, 0:32].reshape(size, CH),
                odd[k].reshape(size, CH),
                even[k, :, 16:48].reshape(size, CH),
            ],
            axis=1,
        )

    lower = sub < 4

    def blend(total, n, width, g, h):
        for c in range(width // 128):
            ct = n // 128 + c
            lanes = pl.ds(ct * 128, 128)
            for p in range(4):
                at = (4 * g + 2 * h + p // 2) * COLS
                for m in range(4):
                    cells = total[p % 2, c, pl.ds(at + 8 * m, 8), :]
                    turn[c, h, p, pl.ds(m, 8, stride=4), :] = cells
            whole = []
            for j in range(STEPS):
                whole.append(sum_d[h, ct, pl.ds((g * STEPS + j) * 16, 16), :].astype(F32))
            for e in range(2):
                parts = [x[8 * e : 8 * e + 8] for x in whole]
                for f in range(2):
                    p = 2 * e + f
                    r = 8 * g + 4 * h + p
                    line = []
                    for v in range(4):
                        a, b = parts[2 * v], parts[2 * v + 1]
                        if f == 0:
                            line.append(jnp.where(lower, a, pltpu.roll(b, 4, 0)))
                        else:
                            line.append(jnp.where(lower, pltpu.roll(a, 4, 0), b))
                    dil = jnp.concatenate(line, axis=0)
                    w = wgt[pl.ds(r * COLS, COLS), :].astype(F32)
                    mixed = w * turn[c, h, p] + (1.0 - w) * dil
                    mixed = mixed.astype(BF16)
                    lhs_d[2 * r, :, lanes] = mixed[0:16]
                    lhs_d[2 * r + 1, :, lanes] = mixed[16:32]

    quarter = PAIRS // 4
    products(
        dilated_lhs, wd, bia_d, 0, 512, total_a, keep_dilated,
        lambda k: form_local(k * quarter, (k + 1) * quarter),
    )
    products(dilated_lhs, wd, bia_d, 512, 128, total_b, keep_dilated)
    products(local_lhs, wl, bia_l, 0, 512, total_a, keep_local(total_a))

    stores = []

    def store(first, last, n, width):
        at, lanes = pl.ds(8 * first, 8 * (last - first)), pl.ds(n, width)
        copy = pltpu.make_async_copy(
            lhs_d.at[at, :, lanes], out.at[at, :, lanes], sem_out.at[len(stores)]
        )
        copy.start()
        stores.append(copy)

    def beside(k):
        for unit in range(3 * k, 3 * k + 3):
            blend(total_a, 0, 512, unit // 2, unit % 2)

    products(
        local_lhs, wl, bia_l, 512, 128, total_b, keep_local(total_b), beside,
        lambda k: store(3 * k, 3 * k + 3, 0, 512),
    )
    for part in range(2):
        for unit in range(6 * part, 6 * part + 6):
            blend(total_b, 512, 128, unit // 2, unit % 2)
        store(6 * part, 6 * part + 6, 512, 128)
    for copy in stores:
        copy.wait()


VM = pl.BlockSpec(memory_space=pltpu.VMEM)
HB = pl.BlockSpec(memory_space=pltpu.HBM)


def per_device(
    latent, blend, gamma_local, beta_local, kernel_local, bias_local,
    gamma_dilated, beta_dilated, kernel_dilated, bias_dilated,
):
    kl = pltpu.with_memory_space_constraint(kernel_local.reshape(3, KDIM, CH), pltpu.HBM)
    kd = pltpu.with_memory_space_constraint(kernel_dilated.reshape(3, KDIM, CH), pltpu.HBM)
    latent = pltpu.with_memory_space_constraint(latent, pltpu.HBM)
    blend = pltpu.with_memory_space_constraint(blend.T, pltpu.HBM)
    dma = pltpu.SemaphoreType.DMA
    gathered = pl.pallas_call(
        gather_kernel,
        out_shape=(
            pltpu.VMEM((UNITS + 2, STEPS + 2, 16, CH), BF16),
            pltpu.VMEM((5, ROWS + 2, 40, 128), F32),
            pltpu.VMEM((48, 128), F32),
            pltpu.VMEM((4, KDIM, CH), BF16),
            pltpu.VMEM((4, KDIM, CH), BF16),
            pltpu.VMEM((ROWS * COLS, 128), BF16),
        ),
        in_specs=[HB, HB, HB, HB],
        out_specs=(VM,) * 6,
        scratch_shapes=[
            pltpu.VMEM((ROWS, COLS, CH), BF16),
            pltpu.VMEM((COLS, ROWS), jnp.int32),
            pltpu.VMEM((KDIM, CH), BF16),
            pltpu.VMEM((KDIM, CH), BF16),
            pltpu.VMEM((8, 128), F32),
            pltpu.VMEM((8, 128), F32),
            pltpu.VMEM((NROW, 8, 128), F32),
            pltpu.VMEM((NCOL, 8, 128), F32),
            dma((PARTS,)), dma, dma((6,)), dma((8,)), dma((8,)),
            dma((NROW,)), dma((NROW,)), dma((NCOL,)), dma((NCOL,)),
        ],
        compiler_params=pltpu.CompilerParams(
            collective_id=0, has_side_effects=True, vmem_limit_bytes=12 * 2**20
        ),
        name="gather",
    )(latent, kl, kd, blend)
    gathered = [pltpu.with_memory_space_constraint(a, pltpu.VMEM) for a in gathered]
    small = (gamma_local, beta_local, bias_local, gamma_dilated, beta_dilated, bias_dilated)
    return pl.pallas_call(
        conv_kernel,
        out_shape=jax.ShapeDtypeStruct((2 * ROWS, 16, CH), BF16),
        in_specs=[VM] * 12,
        out_specs=HB,
        scratch_shapes=[
            pltpu.VMEM((4 * BLOCKS, 16, CH), BF16),
            pltpu.VMEM((4, PAIRS, 48, CH), BF16),
            pltpu.VMEM((4, PAIRS, 32, CH), BF16),
            pltpu.VMEM((2, 5, PAIRS * COLS, 128), BF16),
            pltpu.VMEM((2, 4, PAIRS * COLS, 128), F32),
            pltpu.VMEM((2, 1, PAIRS * COLS, 128), F32),
            pltpu.VMEM((4, 2, 4, COLS, 128), F32),
            pltpu.VMEM((16, CH), F32),
            pltpu.VMEM((16, CH), F32),
            pltpu.VMEM((8, CH), F32),
            pltpu.VMEM((8, CH), F32),
            dma((6,)),
        ],
        compiler_params=pltpu.CompilerParams(vmem_limit_bytes=26 * 2**20 + 2**19),
        name="conv",
    )(*gathered, *small).reshape(ROWS, COLS, CH)


def solution(mesh):
    placed = (P("row", "col", None), P("row", "col"), P(), P(), P(), P(), P(), P(), P(), P())
    return jax.shard_map(
        per_device, mesh=mesh, in_specs=placed, out_specs=P("row", "col", None), check_vma=False
    )
```

```python
import jax
import jax.numpy as jnp
from jax import lax
from jax.experimental import pallas as pl
from jax.experimental.pallas import tpu as pltpu
from jax.sharding import PartitionSpec as P

CH = 640
GROUPS = 32
PER_GROUP = 20
ROWS = 48
COLS = 32
PAIRS = ROWS // 2
KDIM = 3 * CH
F32 = jnp.float32
BF16 = jnp.bfloat16
MESH = pl.DeviceIdType.MESH
NROW = 8
NCOL = 16
UNITS = ROWS // 4
STEPS = COLS // 4
BLOCKS = (UNITS // 2) * (STEPS + 2)
PARTS = 4
LOCAL_COUNT = float(UNITS * STEPS * PER_GROUP)


def groups_to_lanes(first_lane):
    chan = lax.broadcasted_iota(jnp.int32, (CH, 128), 0)
    lane = lax.broadcasted_iota(jnp.int32, (CH, 128), 1) - first_lane
    first = lane * PER_GROUP
    inside = (lane >= 0) & (chan >= first) & (chan < first + PER_GROUP)
    return jnp.where(inside, 1.0, 0.0).astype(F32)


def lanes_to_channels():
    lane = lax.broadcasted_iota(jnp.int32, (128, CH), 0)
    chan = lax.broadcasted_iota(jnp.int32, (128, CH), 1)
    first = lane * PER_GROUP
    return jnp.where((chan >= first) & (chan < first + PER_GROUP), 1.0, 0.0).astype(F32)


def exact_dot(a, b):
    return lax.dot_general(
        a, b, (((1,), (0,)), ((), ())), precision=lax.Precision.HIGHEST, preferred_element_type=F32
    )


def merge(tiles, count):
    number = len(tiles)
    total = tiles[0]
    for tile in tiles[1:]:
        total = total + tile
    average = total * (1.0 / number)
    spread = None
    for tile in tiles:
        gap = tile - average
        spread = gap * gap if spread is None else spread + gap * gap
    lanes = lax.broadcasted_iota(jnp.int32, (8, 128), 1)
    is_mean = (lanes // GROUPS) % 2 == 0
    return jnp.where(is_mean, average, total + count * pltpu.roll(spread, GROUPS, 1))


def gather_kernel(
    lat_hbm, kl_hbm, kd_hbm, blend_hbm,
    xd, xn, stats, wl, wd, wgt,
    lat, blend_ref, mid_l, mid_d, tile1, tile2, got1, got2,
    sem_in, sem_b, sem_w, send_h, recv_h, send1, recv1, send2, recv2,
):
    row = lax.axis_index("row")
    col = lax.axis_index("col")
    has_up = row > 0
    has_dn = row < NROW - 1
    has_lf = col > 0
    has_rt = col < NCOL - 1

    loads = []
    for n in range(PARTS):
        at = pl.ds(n * (ROWS // PARTS), ROWS // PARTS)
        copy = pltpu.make_async_copy(lat_hbm.at[at], lat.at[at], sem_in.at[n])
        copy.start()
        loads.append(copy)
    load_blend = pltpu.make_async_copy(blend_hbm, blend_ref, sem_b)
    load_blend.start()

    barrier = pltpu.get_barrier_semaphore()
    for d in range(1, NROW):
        pl.semaphore_signal(barrier, 1, device_id=(lax.rem(row + d, NROW), col), device_id_type=MESH)
    for d in range(1, NCOL):
        pl.semaphore_signal(barrier, 1, device_id=(row, lax.rem(col + d, NCOL)), device_id_type=MESH)
    for dr, okr in ((-1, has_up), (1, has_dn)):
        for dc, okc in ((-1, has_lf), (1, has_rt)):
            @pl.when(okr & okc)
            def _():
                pl.semaphore_signal(barrier, 1, device_id=(row + dr, col + dc), device_id_type=MESH)

    loads[0].wait()
    cells = jnp.concatenate([lat[p, 0:16, :].astype(F32)[0:4] for p in range(4)], axis=0)
    centre = jnp.dot(
        cells.astype(BF16), groups_to_lanes(0).astype(BF16), preferred_element_type=F32
    )
    centre = (centre * (1.0 / PER_GROUP)).astype(BF16)
    shift = jnp.dot(centre, lanes_to_channels().astype(BF16), preferred_element_type=F32)

    def arrange(u, carry):
        acc, square = carry
        rows = []
        for p in range(4):
            x = lat[4 * u + p].astype(F32)
            for ct in range(5):
                xn[ct, 4 * u + p + 1, pl.ds(0, COLS), :] = x[:, ct * 128 : ct * 128 + 128]
            rows.append(x)
        for j in range(STEPS):
            cells = jnp.concatenate([x[4 * j : 4 * j + 4] for x in rows], axis=0)
            xd[u + 1, j + 1] = cells.astype(BF16)
            gap = cells - shift
            acc = acc + gap
            square = square + gap * gap
        return acc, square

    carry = (jnp.zeros((16, CH), F32), jnp.zeros((16, CH), F32))
    for n in range(PARTS):
        if n:
            loads[n].wait()
        carry = lax.fori_loop(n * UNITS // PARTS, (n + 1) * UNITS // PARTS, arrange, carry)

    weights = []
    for n, (src, planes, mid) in enumerate(((kd_hbm, wd, mid_d), (kl_hbm, wl, mid_l))):
        for m, (a, dst) in enumerate(((0, planes.at[0]), (1, mid), (2, planes.at[3]))):
            copy = pltpu.make_async_copy(src.at[a], dst, sem_w.at[3 * n + m])
            copy.start()
            weights.append(copy)

    both = exact_dot(jnp.concatenate(carry, axis=0), groups_to_lanes(0))
    gap, square = both[0:16], pltpu.roll(both[16:32], GROUPS, 1)
    mean = centre.astype(F32) + gap * (1.0 / LOCAL_COUNT)
    square = square - pltpu.roll(gap * gap, GROUPS, 1) * (1.0 / LOCAL_COUNT)
    lanes = lax.broadcasted_iota(jnp.int32, (16, 128), 1)
    tile = jnp.where(lanes < GROUPS, mean, jnp.where(lanes < 2 * GROUPS, square, 0.0))
    tile1[...] = tile[0:8] + pltpu.roll(tile[8:16], 2 * GROUPS, 1)

    diagonals = (jnp.where(has_up, 1, 0) + jnp.where(has_dn, 1, 0)) * (
        jnp.where(has_lf, 1, 0) + jnp.where(has_rt, 1, 0)
    )
    pl.semaphore_wait(barrier, NROW - 1 + NCOL - 1 + diagonals)

    first = []
    for d in range(1, NROW):
        copy = pltpu.make_async_remote_copy(
            src_ref=tile1, dst_ref=got1.at[d], send_sem=send1.at[d], recv_sem=recv1.at[d],
            device_id=(lax.rem(row + d, NROW), col), device_id_type=MESH,
        )
        copy.start()
        first.append(copy)

    halos = []
    inner_u, inner_j = pl.ds(1, UNITS), pl.ds(1, STEPS)
    for n, (src, dst, dr, dc, ok, got) in enumerate((
        (xd.at[inner_u, STEPS], xd.at[inner_u, 0], 0, 1, has_rt, has_lf),
        (xd.at[inner_u, 1], xd.at[inner_u, STEPS + 1], 0, -1, has_lf, has_rt),
        (xd.at[UNITS, inner_j], xd.at[0, inner_j], 1, 0, has_dn, has_up),
        (xd.at[1, inner_j], xd.at[UNITS + 1, inner_j], -1, 0, has_up, has_dn),
        (xd.at[UNITS, STEPS], xd.at[0, 0], 1, 1, has_dn & has_rt, has_up & has_lf),
        (xd.at[1, STEPS], xd.at[UNITS + 1, 0], -1, 1, has_up & has_rt, has_dn & has_lf),
        (xd.at[UNITS, 1], xd.at[0, STEPS + 1], 1, -1, has_dn & has_lf, has_up & has_rt),
        (xd.at[1, 1], xd.at[UNITS + 1, STEPS + 1], -1, -1, has_up & has_lf, has_dn & has_rt),
    )):
        copy = pltpu.make_async_remote_copy(
            src_ref=src, dst_ref=dst, send_sem=send_h.at[n], recv_sem=recv_h.at[n],
            device_id=(row + dr, col + dc), device_id_type=MESH,
        )
        halos.append((copy, ok, got))
        @pl.when(ok)
        def _():
            copy.start()

    def form(dst, mid):
        @pl.loop(0, KDIM // 32)
        def _(i):
            at = pl.ds(pl.multiple_of(i * 32, 32), 32)
            ends = dst[0, at, :].astype(F32) + dst[3, at, :].astype(F32)
            centre_tap = mid[at, :].astype(F32)
            dst[1, at, :] = ((ends + centre_tap) * 0.5).astype(BF16)
            dst[2, at, :] = ((ends - centre_tap) * 0.5).astype(BF16)

    load_blend.wait()
    turned = blend_ref[...].astype(F32) * 0.25
    for r in range(ROWS):
        wgt[pl.ds(r * COLS, COLS), :] = jnp.broadcast_to(turned[:, r : r + 1], (COLS, 128)).astype(BF16)

    for copy in first:
        copy.wait_recv()
    tile2[...] = merge([tile1[...]] + [got1[d] for d in range(1, NROW)], LOCAL_COUNT)
    second = []
    for d in (10, 6, 9, 7, 11, 5, 2, 14, 8, 3, 13, 1, 15, 4, 12):
        copy = pltpu.make_async_remote_copy(
            src_ref=tile2, dst_ref=got2.at[d], send_sem=send2.at[d], recv_sem=recv2.at[d],
            device_id=(row, lax.rem(col + d, NCOL)), device_id_type=MESH,
        )
        copy.start()
        second.append(copy)

    for copy in weights[:3]:
        copy.wait()
    form(wd, mid_d)

    for copy in weights[3:]:
        copy.wait()
    form(wl, mid_l)

    for copy, ok, got in halos:
        @pl.when(got)
        def _():
            copy.wait_recv()

        @pl.when(ok)
        def _():
            copy.wait_send()

    for src, at in ((0, 0), (UNITS + 1, ROWS + 1)):
        part = 12 if src == 0 else 0
        for j in range(STEPS):
            x = xd[src, j + 1].astype(F32)[part : part + 4]
            for ct in range(5):
                xn[ct, at, pl.ds(4 * j, 4), :] = x[:, ct * 128 : ct * 128 + 128]
    for j, q, at in ((0, 3, COLS + 1), (STEPS + 1, 0, COLS)):
        @pl.loop(0, UNITS)
        def _(u):
            x = xd[u + 1, j].astype(F32)
            for p in range(4):
                for ct in range(5):
                    cell = x[4 * p + q : 4 * p + q + 1, ct * 128 : ct * 128 + 128]
                    xn[ct, 4 * u + p + 1, pl.ds(at, 1), :] = cell
        for src, p, r in ((0, 3, 0), (UNITS + 1, 0, ROWS + 1)):
            x = xd[src, j].astype(F32)
            for ct in range(5):
                cell = x[4 * p + q : 4 * p + q + 1, ct * 128 : ct * 128 + 128]
                xn[ct, r, pl.ds(at, 1), :] = cell

    for copy in second:
        copy.wait_recv()
    tile = merge([tile2[...]] + [got2[d] for d in range(1, NCOL)], LOCAL_COUNT * NROW)
    tile = jnp.concatenate([tile, pltpu.roll(tile, 2 * GROUPS, 1)], axis=0)
    count = LOCAL_COUNT * NROW * NCOL
    square = pltpu.roll(tile, 128 - GROUPS, 1)

    def everywhere(v):
        return jnp.broadcast_to(jnp.sum(v, axis=0, keepdims=True), (8, 128)) * (1.0 / 16.0)

    var = jnp.where(lanes < GROUPS, square * (1.0 / count), 0.0)
    tile = jnp.where(lanes < GROUPS, tile, 0.0)
    mean_all = everywhere(tile)
    gap = tile - mean_all[0:1]
    stats[pl.ds(0, 16)] = tile
    stats[pl.ds(16, 16)] = lax.rsqrt(var + 1e-05)
    stats[pl.ds(32, 8)] = mean_all
    stats[pl.ds(40, 8)] = lax.rsqrt(everywhere(var + gap * gap) + 1e-05)

    for copy in first + second:
        copy.wait_send()


def conv_kernel(
    xd, xn, stats, wl, wd, wgt,
    gam_l, bet_l, bia_l, gam_d, bet_d, bia_d,
    out,
    lhs_d, even, odd, sum_d, total_a, total_b, turn, scale_d, shift_d, scale_l, shift_l,
    sem_out,
):
    row = lax.axis_index("row")
    col = lax.axis_index("col")
    has_up = row > 0
    has_dn = row < NROW - 1
    has_lf = col > 0
    has_rt = col < NCOL - 1

    spread = exact_dot(stats[...], lanes_to_channels())
    for n, gam, bet, scale, shift in (
        (0, gam_d, bet_d, scale_d, shift_d), (32, gam_l, bet_l, scale_l, shift_l)
    ):
        rows = 16 if n == 0 else 8
        by = spread[n + rows : n + 2 * rows] * (gam[...].reshape(1, CH) * 0.5)
        scale[...] = by
        shift[...] = bet[...].reshape(1, CH) * 0.5 - spread[n : n + rows] * by

    def silu(x, scale, shift):
        h = x * scale + shift
        return h + h * jnp.tanh(h)

    def mix(d0, d1, d2, d3):
        return (d0 - d2, d1 + d2, d2 - d1, d1 - d3)

    @pl.loop(0, STEPS + 2)
    def _(j):
        for ct in range(5):
            lanes = pl.ds(ct * 128, 128)
            by, plus = scale_d[:, lanes], shift_d[:, lanes]

            def unit(u):
                return silu(xd[u, j, :, lanes].astype(F32), by, plus)

            d0 = jnp.where(has_up, unit(0), 0.0)
            d1 = unit(1)
            for n in range(UNITS // 2):
                d2 = unit(2 * n + 2)
                d3 = unit(2 * n + 3)
                if n == UNITS // 2 - 1:
                    d3 = jnp.where(has_dn, d3, 0.0)
                for k, v in enumerate(mix(d0, d1, d2, d3)):
                    lhs_d[k * BLOCKS + n * (STEPS + 2) + j, :, lanes] = v.astype(BF16)
                d0, d1 = d2, d3

    for j, ok in ((0, has_lf), (STEPS + 1, has_rt)):
        @pl.when(jnp.logical_not(ok))
        def _():
            for k in range(4):
                for n in range(UNITS // 2):
                    lhs_d[k * BLOCKS + n * (STEPS + 2) + j] = jnp.zeros((16, CH), BF16)

    sub = lax.broadcasted_iota(jnp.int32, (8, 128), 0)
    first = sub == 0
    keep_rt = (sub < 7) | has_rt

    def form_local(t0, t1):
        for ct in range(5):
            lanes = pl.ds(ct * 128, 128)
            by, plus = scale_l[:, lanes], shift_l[:, lanes]

            def line(r):
                cells = [silu(xn[ct, r, pl.ds(m, 8, stride=4), :], by, plus) for m in range(5)]
                cells[4] = jnp.where(keep_rt, cells[4], 0.0)
                edge = silu(jnp.broadcast_to(xn[ct, r, pl.ds(COLS + 1, 1), :], (8, 128)), by, plus)
                edge = jnp.where(has_lf, edge, 0.0)
                cells.insert(0, jnp.where(first, edge, pltpu.roll(cells[3], 1, 0)))
                if r == 0:
                    cells = [jnp.where(has_up, v, 0.0) for v in cells]
                if r == ROWS + 1:
                    cells = [jnp.where(has_dn, v, 0.0) for v in cells]
                return cells

            d0, d1 = line(2 * t0), line(2 * t0 + 1)
            for t in range(t0, t1):
                d2, d3 = line(2 * t + 2), line(2 * t + 3)
                mixed = [mix(*quad) for quad in zip(d0, d1, d2, d3)]
                for k in range(4):
                    for half in range(3):
                        v = jnp.concatenate([mixed[2 * half][k], mixed[2 * half + 1][k]], axis=0)
                        even[k, t, pl.ds(16 * half, 16), lanes] = v.astype(BF16)
                    for half in range(2):
                        v = jnp.concatenate([mixed[2 * half + 1][k], mixed[2 * half + 2][k]], axis=0)
                        odd[k, t, pl.ds(16 * half, 16), lanes] = v.astype(BF16)
                d0, d1 = d2, d3

    size = PAIRS * COLS

    def products(get, planes, bias, n, width, total, keep, beside=None, after=None):
        at = pl.ds(n, width)
        for k in range(4):
            m = jnp.dot(get(k), planes[k, :, at], preferred_element_type=F32)
            if beside is not None:
                beside(k)
            for c in range(width // 128):
                ct = n // 128 + c
                v = m[:, c * 128 : c * 128 + 128]
                if k == 0:
                    total[0, c] = v + bias[pl.ds(ct * 128, 128)].reshape(1, 128)
                elif k == 1:
                    total[0, c] += v
                    total[1, c] = v + bias[pl.ds(ct * 128, 128)].reshape(1, 128)
                elif k == 2:
                    keep(0, c, ct, total[0, c] + v)
                    total[1, c] -= v
                else:
                    keep(1, c, ct, total[1, c] - v)
            if after is not None:
                after(k)

    def keep_dilated(h, c, ct, v):
        sum_d[h, ct] = v.astype(BF16)

    def keep_local(total):
        def keep(h, c, ct, v):
            total[h, c] = v

        return keep

    def dilated_lhs(k):
        taps = []
        for b in range(3):
            lines = [
                lhs_d[pl.ds(k * BLOCKS + n * (STEPS + 2) + b, STEPS)] for n in range(UNITS // 2)
            ]
            taps.append(jnp.concatenate(lines, axis=0).reshape(size, CH))
        return jnp.concatenate(taps, axis=1)

    def local_lhs(k):
        return jnp.concatenate(
            [
                even[k, :, 0:32].reshape(size, CH),
                odd[k].reshape(size, CH),
                even[k, :, 16:48].reshape(size, CH),
            ],
            axis=1,
        )

    lower = sub < 4

    def blend(total, n, width, g, h):
        for c in range(width // 128):
            ct = n // 128 + c
            lanes = pl.ds(ct * 128, 128)
            for p in range(4):
                at = (4 * g + 2 * h + p // 2) * COLS
                for m in range(4):
                    cells = total[p % 2, c, pl.ds(at + 8 * m, 8), :]
                    turn[c, h, p, pl.ds(m, 8, stride=4), :] = cells
            whole = []
            for j in range(STEPS):
                whole.append(sum_d[h, ct, pl.ds((g * STEPS + j) * 16, 16), :].astype(F32))
            for e in range(2):
                parts = [x[8 * e : 8 * e + 8] for x in whole]
                for f in range(2):
                    p = 2 * e + f
                    r = 8 * g + 4 * h + p
                    line = []
                    for v in range(4):
                        a, b = parts[2 * v], parts[2 * v + 1]
                        if f == 0:
                            line.append(jnp.where(lower, a, pltpu.roll(b, 4, 0)))
                        else:
                            line.append(jnp.where(lower, pltpu.roll(a, 4, 0), b))
                    dil = jnp.concatenate(line, axis=0)
                    w = wgt[pl.ds(r * COLS, COLS), :].astype(F32)
                    mixed = w * turn[c, h, p] + (1.0 - w) * dil
                    mixed = mixed.astype(BF16)
                    lhs_d[2 * r, :, lanes] = mixed[0:16]
                    lhs_d[2 * r + 1, :, lanes] = mixed[16:32]

    quarter = PAIRS // 4
    products(
        dilated_lhs, wd, bia_d, 0, 512, total_a, keep_dilated,
        lambda k: form_local(k * quarter, (k + 1) * quarter),
    )
    products(dilated_lhs, wd, bia_d, 512, 128, total_b, keep_dilated)
    products(local_lhs, wl, bia_l, 0, 512, total_a, keep_local(total_a))

    stores = []

    def store(first, last, n, width):
        at, lanes = pl.ds(8 * first, 8 * (last - first)), pl.ds(n, width)
        copy = pltpu.make_async_copy(
            lhs_d.at[at, :, lanes], out.at[at, :, lanes], sem_out.at[len(stores)]
        )
        copy.start()
        stores.append(copy)

    def beside(k):
        for unit in range(3 * k, 3 * k + 3):
            blend(total_a, 0, 512, unit // 2, unit % 2)

    products(
        local_lhs, wl, bia_l, 512, 128, total_b, keep_local(total_b), beside,
        lambda k: store(3 * k, 3 * k + 3, 0, 512),
    )
    for part in range(2):
        for unit in range(6 * part, 6 * part + 6):
            blend(total_b, 512, 128, unit // 2, unit % 2)
        store(6 * part, 6 * part + 6, 512, 128)
    for copy in stores:
        copy.wait()


VM = pl.BlockSpec(memory_space=pltpu.VMEM)
HB = pl.BlockSpec(memory_space=pltpu.HBM)


def per_device(
    latent, blend, gamma_local, beta_local, kernel_local, bias_local,
    gamma_dilated, beta_dilated, kernel_dilated, bias_dilated,
):
    kl = pltpu.with_memory_space_constraint(kernel_local.reshape(3, KDIM, CH), pltpu.HBM)
    kd = pltpu.with_memory_space_constraint(kernel_dilated.reshape(3, KDIM, CH), pltpu.HBM)
    latent = pltpu.with_memory_space_constraint(latent, pltpu.HBM)
    blend = pltpu.with_memory_space_constraint(blend.T, pltpu.HBM)
    dma = pltpu.SemaphoreType.DMA
    gathered = pl.pallas_call(
        gather_kernel,
        out_shape=(
            pltpu.VMEM((UNITS + 2, STEPS + 2, 16, CH), BF16),
            pltpu.VMEM((5, ROWS + 2, 40, 128), F32),
            pltpu.VMEM((48, 128), F32),
            pltpu.VMEM((4, KDIM, CH), BF16),
            pltpu.VMEM((4, KDIM, CH), BF16),
            pltpu.VMEM((ROWS * COLS, 128), BF16),
        ),
        in_specs=[HB, HB, HB, HB],
        out_specs=(VM,) * 6,
        scratch_shapes=[
            pltpu.VMEM((ROWS, COLS, CH), BF16),
            pltpu.VMEM((COLS, ROWS), jnp.int32),
            pltpu.VMEM((KDIM, CH), BF16),
            pltpu.VMEM((KDIM, CH), BF16),
            pltpu.VMEM((8, 128), F32),
            pltpu.VMEM((8, 128), F32),
            pltpu.VMEM((NROW, 8, 128), F32),
            pltpu.VMEM((NCOL, 8, 128), F32),
            dma((PARTS,)), dma, dma((6,)), dma((8,)), dma((8,)),
            dma((NROW,)), dma((NROW,)), dma((NCOL,)), dma((NCOL,)),
        ],
        compiler_params=pltpu.CompilerParams(
            collective_id=0, has_side_effects=True, vmem_limit_bytes=12 * 2**20
        ),
        name="gather",
    )(latent, kl, kd, blend)
    gathered = [pltpu.with_memory_space_constraint(a, pltpu.VMEM) for a in gathered]
    small = (gamma_local, beta_local, bias_local, gamma_dilated, beta_dilated, bias_dilated)
    return pl.pallas_call(
        conv_kernel,
        out_shape=jax.ShapeDtypeStruct((2 * ROWS, 16, CH), BF16),
        in_specs=[VM] * 12,
        out_specs=HB,
        scratch_shapes=[
            pltpu.VMEM((4 * BLOCKS, 16, CH), BF16),
            pltpu.VMEM((4, PAIRS, 48, CH), BF16),
            pltpu.VMEM((4, PAIRS, 32, CH), BF16),
            pltpu.VMEM((2, 5, PAIRS * COLS, 128), BF16),
            pltpu.VMEM((2, 4, PAIRS * COLS, 128), F32),
            pltpu.VMEM((2, 1, PAIRS * COLS, 128), F32),
            pltpu.VMEM((4, 2, 4, COLS, 128), F32),
            pltpu.VMEM((16, CH), F32),
            pltpu.VMEM((16, CH), F32),
            pltpu.VMEM((8, CH), F32),
            pltpu.VMEM((8, CH), F32),
            dma((6,)),
        ],
        compiler_params=pltpu.CompilerParams(vmem_limit_bytes=26 * 2**20 + 2**19),
        name="conv",
    )(*gathered, *small).reshape(ROWS, COLS, CH)


def solution(mesh):
    placed = (P("row", "col", None), P("row", "col"), P(), P(), P(), P(), P(), P(), P(), P())
    return jax.shard_map(
        per_device, mesh=mesh, in_specs=placed, out_specs=P("row", "col", None), check_vma=False
    )
```
